256 devices in a mesh: layer: 8 (over z_lo, x), lat: 32 (over z_hi, y, core).
Axes of the slice: x: 4, y: 4, z: 8 (z_hi: 4, z_lo: 2; z = z_hi * 2 + z_lo), core: 2. Of those that a mesh axis runs over, the one named last changes fastest.
Arguments:
- acts: bfloat16 [8, 512, 1280], P('layer', 'lat'), may hold values from -6 to 6
- enc_weight: bfloat16 [8, 1280, 8192], P('layer', None, 'lat'), may hold values from -0.15625 to 0.15625
- enc_bias: float32 [8, 8192], P('layer', 'lat'), may hold values from -3 to 3
- dec_weight: bfloat16 [8, 8, 8192, 1280], P('layer', None, 'lat'), may hold values from -0.0625 to 0.0625
- dec_bias: float32 [8, 1280], P('layer'), may hold values from -3 to 3
Outputs:
- recon: bfloat16 [8, 512, 1280], P('layer', 'lat')
The draws below stay inside these ranges and needn't reach their ends.
All inputs are finite; a program needn't handle non-finite values.
Results may differ from the reference program's by a relative error of at most 0.0048.
Values may be sent and summed in bfloat16 or wider, within the bound.
A program may use at most 128 MiB of HBM per device.

```python
import jax
import jax.numpy as jnp

D = 1280
LATENTS = 8192
TOKENS = 512
LAYERS = 8


def levels(key, shape, cuts, low, largest):
    factor_of = 1.0
    for position, blocks in cuts:
        steps = jax.random.uniform(jax.random.fold_in(jax.random.fold_in(key, 6), position), (blocks,), jnp.float32, low / len(cuts), largest / len(cuts))
        factor_of = factor_of * jnp.repeat(jnp.exp(steps), shape[position] // blocks).reshape((-1,) + (1,) * (len(shape) - 1 - position))
    return factor_of


def normal_values(stream_key, extent, spread, limit, cuts=(), held_as=jnp.bfloat16):
    factor_of = levels(stream_key, extent, cuts, -0.22, 0.18) if cuts else 1.0
    result = jax.random.normal(stream_key, extent, jnp.float32) * spread * factor_of
    return jnp.minimum(jnp.maximum(result, -limit), limit).astype(held_as)


def setup_inputs(seed: int = 0) -> dict:
    splits = jax.random.split(jax.random.key(seed), 6)
    acts = normal_values(splits[0], (LAYERS, TOKENS, D), 1.0, 6.0, ((0, 8), (1, 32)))
    enc_weight = normal_values(splits[1], (LAYERS, D, LATENTS), D ** -0.5, 0.15625, ((0, 8), (2, 32)))
    enc_bias = normal_values(splits[2], (LAYERS, LATENTS), 0.5, 3.0, ((0, 8), (1, 32)), jnp.float32)
    dec_weight = normal_values(splits[3], (LAYERS, LAYERS, LATENTS, D), LATENTS ** -0.5, 0.0625, ((0, 8), (2, 32)))
    dec_bias = normal_values(splits[4], (LAYERS, D), 0.5, 3.0, ((0, 8),), jnp.float32)
    return {"acts": acts, "enc_weight": enc_weight, "enc_bias": enc_bias, "dec_weight": dec_weight, "dec_bias": dec_bias}


def reference(acts, enc_weight, enc_bias, dec_weight, dec_bias):
    latents = []
    for source in range(LAYERS):
        pre = jnp.dot(acts[source], enc_weight[source], preferred_element_type=jnp.float32) + enc_bias[source]
        latents.append(jnp.maximum(pre, 0.0).astype(jnp.bfloat16))
    results = []
    for target in range(LAYERS):
        total = jnp.zeros((TOKENS, D), jnp.float32)
        for source in range(target + 1):
            total = total + jnp.dot(latents[source], dec_weight[source, target], preferred_element_type=jnp.float32)
        results.append((total + dec_bias[target][None, :]).astype(jnp.bfloat16))
    return jnp.stack(results, axis=0)
```

```python
import functools

import jax
import jax.numpy as jnp
from jax import lax
from jax.experimental import pallas as pl
from jax.experimental.pallas import tpu as pltpu
from jax.sharding import PartitionSpec as P

PLAN = [
    [(1, [(0, 1)]), (3, [(0, 1)]), (0, [(0, 1)]), (2, [(0, 1), (1, 1)])],
    [(4, [(1, 1)]), (7, [(1, 1)]), (1, [(1, 1)]), (6, [(1, 1), (0, 1)])],
    [(4, [(2, 1)]), (2, [(2, 1)]), (3, [(2, 1), (1, 1)]), (6, [(2, 1), (3, 1)])],
    [(4, [(3, 1)]), (7, [(3, 1)]), (3, [(3, 1)]), (5, [(3, 1), (0, 1), (2, 1)])],
    [(7, [(4, 1), (0, 1)]), (4, [(4, 1), (0, -1)])],
    [(6, [(5, 1)]), (5, [(5, 1), (1, 1), (4, 1)])],
    [(6, [(6, 1)]), (7, [(6, 1), (2, -1), (5, 1)])],
    [(7, [(7, 1)]), (6, [(4, 1)])],
]

F32, BF16 = jnp.float32, jnp.bfloat16
MESH = pl.DeviceIdType.MESH


class Tables:
    def __init__(self, plan):
        n = len(plan)
        self.n = n
        self.tasks = [[(l, z, m, t) for t, (m, ls) in enumerate(plan[p]) for l, z in ls] for p in range(n)]
        self.targets = max(len(plan[p]) for p in range(n))
        self.depth = max(len(k) for k in self.tasks)
        self.ntargets = [len(plan[p]) for p in range(n)]
        self.target = [[m for m, _ in plan[p]] for p in range(n)]
        self.start = [[min(k for k, task in enumerate(self.tasks[p]) if task[3] == t) for t in range(len(plan[p]))] for p in range(n)]
        self.stop = [[max(k for k, task in enumerate(self.tasks[p]) if task[3] == t) + 1 for t in range(len(plan[p]))] for p in range(n)]
        self.sources = []
        for p in range(n):
            seen = []
            for l, z, _, _ in self.tasks[p]:
                if l != p and (l, z) not in seen:
                    seen.append((l, z))
            self.sources.append(seen)
        self.task_latent = [[0 if l == p else 1 + self.sources[p].index((l, z)) for l, z, _, _ in self.tasks[p]] for p in range(n)]
        self.task_new = [[int(s > 0 and s not in self.task_latent[p][:k]) for k, s in enumerate(self.task_latent[p])] for p in range(n)]
        self.task_target = [[m for _, _, m, _ in self.tasks[p]] for p in range(n)]
        self.dec = [[(p, z, m, k) for k in range(self.depth) for p in range(n) for kk, (a, z, m, _) in enumerate(self.tasks[p]) if a == l != p and kk == k] for l in range(n)]
        self.lat = [[(p, z, 1 + s) for p in range(n) for s, (a, z) in enumerate(self.sources[p]) if a == l] for l in range(n)]
        self.adders = [[m] + [p for p in range(n) if p != m and m in self.target[p]] for m in range(n)]
        self.most_adders = max(len(a) for a in self.adders)
        self.adder_slot = [[self.adders[m].index(p) for m in self.target[p]] for p in range(n)]
        for p in range(n):
            assert p in self.target[p] and len(self.tasks[p]) <= 8


def word(values):
    total = sum(v << (4 * i) for i, v in enumerate(values))
    return total - (1 << 32) if total >= 1 << 31 else total


def pick(index, values):
    result = jnp.int32(values[0])
    for i, value in enumerate(values[1:], 1):
        result = jnp.where(index == i, jnp.int32(value), result)
    return result


def words(index, lists):
    return pick(index, [word(values) for values in lists])


def nibble(packed, i):
    return lax.bitwise_and(lax.shift_right_logical(packed, jnp.int32(4 * i)), jnp.int32(15))


def kernel(
    tab, acts, enc, enc_bias, dec, dec_bias, out,
    every, enc_v, latents, decs, acc, core_out, core_in, y_out, y_own, y_in, z_out, z_own, z_in,
    s_in, s_dec, s_task, r_task, s_lat, r_lat, s_gz, r_gz, s_gy, r_gy, s_gc, r_gc,
    s_core, r_core, s_y, r_y, s_z, r_z,
):
    me = lax.axis_index("layer")
    lat = lax.axis_index("lat")
    zh, y, c = lat // 8, (lat // 2) % 4, lat % 2
    width = acts.shape[2]

    def device(layer, zh_, y_, c_):
        return (layer, (zh_ % 4) * 8 + (y_ % 4) * 2 + c_)

    def remote(src, dst, send, recv, where):
        return pltpu.make_async_remote_copy(
            src_ref=src, dst_ref=dst, send_sem=send, recv_sem=recv, device_id=where, device_id_type=MESH
        )

    def rows(start, size):
        return pl.ds(pl.multiple_of(start, 16), size)

    n_targets = pick(me, tab.ntargets)
    n_tasks = pick(me, [len(k) for k in tab.tasks])
    w_target = words(me, tab.target)
    w_start = words(me, tab.start)
    w_stop = words(me, tab.stop)
    w_task_lat = words(me, tab.task_latent)
    w_task_new = words(me, tab.task_new)
    w_task_m = words(me, tab.task_target)
    n_dec = pick(me, [len(d) for d in tab.dec])
    w_dec_p = words(me, [[d[0] for d in ds] for ds in tab.dec])
    w_dec_z = words(me, [[int(d[1] < 0) for d in ds] for ds in tab.dec])
    w_dec_m = words(me, [[d[2] for d in ds] for ds in tab.dec])
    w_dec_k = words(me, [[d[3] for d in ds] for ds in tab.dec])
    n_lat = pick(me, [len(d) for d in tab.lat])
    w_lat_p = words(me, [[d[0] for d in ds] for ds in tab.lat])
    w_lat_z = words(me, [[int(d[1] < 0) for d in ds] for ds in tab.lat])
    w_lat_s = words(me, [[d[2] for d in ds] for ds in tab.lat])
    n_src = pick(me, [len(d) for d in tab.sources])
    w_src_l = words(me, [[d[0] for d in ds] for ds in tab.sources])
    w_src_z = words(me, [[int(d[1] < 0) for d in ds] for ds in tab.sources])
    n_add = pick(me, [len(d) for d in tab.adders])
    w_add_p = words(me, tab.adders)
    w_slot = words(me, tab.adder_slot)

    own_block = c * 16 + y * 4 + zh
    in_acts = pltpu.make_async_copy(acts.at[0], every.at[rows(own_block * 16, 16)], s_in.at[0])
    in_enc = pltpu.make_async_copy(enc.at[0], enc_v, s_in.at[1])
    in_acts.start()
    in_enc.start()

    def local_dec(k):
        return pltpu.make_async_copy(dec.at[0, nibble(w_task_m, k)], decs.at[k], s_dec.at[k])

    @pl.loop(0, n_tasks)
    def _(k):
        @pl.when(nibble(w_task_lat, k) == 0)
        def _():
            local_dec(k).start()

    barrier = pltpu.get_barrier_semaphore()

    def greet(where):
        pl.semaphore_signal(barrier, inc=1, device_id=where, device_id_type=MESH)

    greet(device(me, zh, y, 1 - c))
    for step in (1, 2, 3):
        greet(device(me, zh + step, y, c))
        greet(device(me, zh, y + step, c))

    @pl.loop(0, n_src)
    def _(i):
        greet(device(nibble(w_src_l, i), zh + nibble(w_src_z, i), y, c))

    @pl.loop(1, n_add)
    def _(i):
        for step in range(4):
            greet(device(nibble(w_add_p, i), zh + step, y, c))

    in_acts.wait()
    pl.semaphore_wait(barrier, 7 + n_lat + 4 * (n_targets - 1))

    def gather_z(step):
        block = every.at[rows(own_block * 16, 16)]
        return remote(block, block, s_gz.at[step - 1], r_gz.at[step - 1], device(me, zh + step, y, c))

    def gather_y(step):
        block = every.at[rows(c * 256 + y * 64, 64)]
        return remote(block, block, s_gy.at[step - 1], r_gy.at[step - 1], device(me, zh, y + step, c))

    def gather_c(step):
        block = every.at[rows(c * 256 + ((y + 4 - step) % 4) * 64, 64)]
        return remote(block, block, s_gc.at[step], r_gc.at[step], device(me, zh, y, 1 - c))

    for step in (2, 1, 3):
        gather_z(step).start()

    def send_dec(j):
        k = nibble(w_dec_k, j)
        return remote(
            dec.at[0, nibble(w_dec_m, j)], decs.at[k], s_task.at[j], r_task.at[k],
            device(nibble(w_dec_p, j), zh + 4 - nibble(w_dec_z, j), y, c),
        )

    @pl.loop(0, n_dec)
    def _(j):
        send_dec(j).start()

    for step in (1, 2, 3):
        gather_z(step).wait_recv()
    for step in (2, 1, 3):
        gather_y(step).start()
    gather_c(0).start()
    for step in (1, 3, 2):
        gather_y(step).wait_recv()
        gather_c(step).start()
    in_enc.wait()

    def encode(half):
        pre = jnp.dot(every[rows(half * 256, 256), :], enc_v[...], preferred_element_type=F32) + enc_bias[...]
        latents[0, rows(half * 256, 256), :] = jnp.maximum(pre, 0.0).astype(BF16)

    def send_latent(i, part):
        half = c if part == 0 else 1 - c
        s = nibble(w_lat_s, i)
        return remote(
            latents.at[0, rows(half * 256, 256)], latents.at[s, rows(half * 256, 256)],
            s_lat.at[i, part], r_lat.at[s, part],
            device(nibble(w_lat_p, i), zh + 4 - nibble(w_lat_z, i), y, c),
        )

    encode(c)

    @pl.loop(0, n_lat)
    def _(i):
        send_latent(i, 0).start()

    for step in range(4):
        gather_c(step).wait_recv()
    encode(1 - c)

    @pl.loop(0, n_lat)
    def _(i):
        send_latent(i, 1).start()

    def recv_latent(s, part):
        half = c if part == 0 else 1 - c
        block = latents.at[s, rows(half * 256, 256)]
        return remote(block, block, s_lat.at[0, part], r_lat.at[s, part], device(me, zh, y, 1 - c))

    def recv_dec(k):
        return remote(decs.at[k], decs.at[k], s_task.at[0], r_task.at[k], device(me, zh, y, 1 - c))

    def core_copy(t):
        return remote(core_out.at[t], core_in.at[t], s_core.at[t], r_core.at[t], device(me, zh, y, 1 - c))

    def y_copy(t, step):
        return remote(
            y_out.at[t, rows(((y + step) % 4) * 64, 64)], y_in.at[t, step - 1],
            s_y.at[t, step - 1], r_y.at[t, step - 1], device(me, zh, y + step, c),
        )

    def multiply(t):
        start = nibble(w_start, t)

        @pl.loop(start, nibble(w_stop, t))
        def _(k):
            s = nibble(w_task_lat, k)

            @pl.when(s == 0)
            def _():
                local_dec(k).wait()

            @pl.when(nibble(w_task_new, k) == 1)
            def _():
                recv_latent(s, 0).wait_recv()
                recv_latent(s, 1).wait_recv()

            @pl.when(s > 0)
            def _():
                recv_dec(k).wait_recv()

            @pl.loop(0, width // 256)
            def _(i):
                columns = pl.ds(pl.multiple_of(i * 256, 256), 256)
                term = jnp.dot(latents[s], decs[k, :, columns], preferred_element_type=F32)

                @pl.when(k == start)
                def _():
                    acc[t, :, columns] = term

                @pl.when(k > start)
                def _():
                    acc[t, :, columns] += term

        @pl.loop(0, 4)
        def _(i):
            core_out[t, rows(i * 64, 64), :] = acc[t, rows((1 - c) * 256 + i * 64, 64), :].astype(BF16)

        core_copy(t).start()

    def over_cores(t):
        core_copy(t).wait_recv()

        def total(i):
            return acc[t, rows(c * 256 + i * 64, 64), :] + core_in[t, rows(i * 64, 64), :].astype(F32)

        for step in (2, 1, 3):
            i = (y + step) % 4
            y_out[t, rows(i * 64, 64), :] = total(i).astype(BF16)
            y_copy(t, step).start()
        y_own[t] = total(y)

    def z_copy(t, step):
        m = nibble(w_target, t)
        to = (zh + step) % 4
        return remote(
            z_out.at[t, rows(to * 16, 16)], z_in.at[nibble(w_slot, t), zh], s_z.at[t, step],
            r_z.at[nibble(w_slot, t), zh], device(m, to, y, c),
        )

    def over_y(t):
        total = y_own[t]
        for step in (1, 3, 2):
            y_copy(t, step).wait_recv()
            total = total + y_in[t, step - 1].astype(F32)
        z_out[t] = total.astype(BF16)
        y_own[t] = total

        for step in (2, 1, 3):
            z_copy(t, step).start()

        @pl.when(nibble(w_target, t) != me)
        def _():
            z_copy(t, 0).start()

        @pl.when(nibble(w_target, t) == me)
        def _():
            z_own[...] = y_own[t, rows(zh * 16, 16), :]

    @pl.loop(0, tab.targets + 2)
    def _(i):
        @pl.when(i < n_targets)
        def _():
            multiply(i)

        @pl.when((i >= 1) & (i - 1 < n_targets))
        def _():
            over_cores(i - 1)

        @pl.when((i >= 2) & (i - 2 < n_targets))
        def _():
            over_y(i - 2)

    def recv_z(a, from_zh):
        block = z_in.at[a, from_zh]
        return remote(block, block, s_z.at[0, 0], r_z.at[a, from_zh], device(me, zh, y, 1 - c))

    for step in (1, 2, 3):
        recv_z(0, (zh + step) % 4).wait_recv()
        z_own[...] += z_in[0, (zh + step) % 4].astype(F32)

    @pl.loop(1, n_add)
    def _(a):
        for step in range(4):
            recv_z(a, step).wait_recv()
            z_own[...] += z_in[a, step].astype(F32)

    out[0] = (z_own[...] + dec_bias[...]).astype(BF16)

    for step in (1, 2, 3):
        gather_z(step).wait_send()
        gather_y(step).wait_send()
    for step in range(4):
        gather_c(step).wait_send()

    @pl.loop(0, n_dec)
    def _(j):
        send_dec(j).wait_send()

    @pl.loop(0, n_lat)
    def _(i):
        send_latent(i, 0).wait_send()
        send_latent(i, 1).wait_send()

    @pl.loop(0, n_targets)
    def _(t):
        core_copy(t).wait_send()
        for step in (1, 2, 3):
            y_copy(t, step).wait_send()
            z_copy(t, step).wait_send()

        @pl.when(nibble(w_target, t) != me)
        def _():
            z_copy(t, 0).wait_send()


def solution(mesh):
    tab = Tables(PLAN)
    n_lat = 1 + max(len(s) for s in tab.sources)
    T, K, A = tab.targets, tab.depth, tab.most_adders
    J = max(max(len(d) for d in tab.dec), 1)
    N = max(max(len(d) for d in tab.lat), 1)
    DMA = pltpu.SemaphoreType.DMA

    def local(acts, enc_weight, enc_bias, dec_weight, dec_bias):
        width = acts.shape[2]
        return pl.pallas_call(
            functools.partial(kernel, tab),
            out_shape=jax.ShapeDtypeStruct((1, 16, width), BF16),
            in_specs=[
                pl.BlockSpec(memory_space=pl.ANY),
                pl.BlockSpec(memory_space=pl.ANY),
                pl.BlockSpec(memory_space=pltpu.VMEM),
                pl.BlockSpec(memory_space=pl.ANY),
                pl.BlockSpec(memory_space=pltpu.VMEM),
            ],
            out_specs=pl.BlockSpec(memory_space=pltpu.VMEM),
            scratch_shapes=[
                pltpu.VMEM((512, width), BF16),
                pltpu.VMEM((width, 256), BF16),
                pltpu.VMEM((n_lat, 512, 256), BF16),
                pltpu.VMEM((K, 256, width), BF16),
                pltpu.VMEM((T, 512, width), F32),
                pltpu.VMEM((T, 256, width), BF16),
                pltpu.VMEM((T, 256, width), BF16),
                pltpu.VMEM((T, 256, width), BF16),
                pltpu.VMEM((T, 64, width), F32),
                pltpu.VMEM((T, 3, 64, width), BF16),
                pltpu.VMEM((T, 64, width), BF16),
                pltpu.VMEM((16, width), F32),
                pltpu.VMEM((A, 4, 16, width), BF16),
                DMA((2,)),
                DMA((K,)),
                DMA((J,)),
                DMA((K,)),
                DMA((N, 2)),
                DMA((n_lat, 2)),
                DMA((3,)),
                DMA((3,)),
                DMA((3,)),
                DMA((3,)),
                DMA((4,)),
                DMA((4,)),
                DMA((T,)),
                DMA((T,)),
                DMA((T, 3)),
                DMA((T, 3)),
                DMA((T, 4)),
                DMA((A, 4)),
            ],
            compiler_params=pltpu.CompilerParams(
                collective_id=0, has_side_effects=True, vmem_limit_bytes=60 * 2**20
            ),
        )(acts, enc_weight, enc_bias, dec_weight, dec_bias)

    return jax.shard_map(
        local,
        mesh=mesh,
        in_specs=(
            P("layer", "lat", None),
            P("layer", None, "lat"),
            P("layer", "lat"),
            P("layer", None, "lat", None),
            P("layer", None),
        ),
        out_specs=P("layer", "lat", None),
        check_vma=False,
    )
```

```python
import functools

import jax
import jax.numpy as jnp
from jax import lax
from jax.experimental import pallas as pl
from jax.experimental.pallas import tpu as pltpu
from jax.sharding import PartitionSpec as P

PLAN = [
    [(1, [(0, 1)]), (3, [(0, 1)]), (0, [(0, 1)]), (2, [(0, 1), (1, 1)])],
    [(4, [(1, 1)]), (7, [(1, 1)]), (1, [(1, 1)]), (6, [(1, 1), (0, 1)])],
    [(4, [(2, 1)]), (2, [(2, 1)]), (3, [(2, 1), (1, 1)]), (6, [(2, 1), (3, 1)])],
    [(4, [(3, 1)]), (7, [(3, 1)]), (3, [(3, 1)]), (5, [(3, 1), (0, 1), (2, 1)])],
    [(7, [(4, 1), (0, 1)]), (4, [(4, 1), (0, -1)])],
    [(6, [(5, 1)]), (5, [(5, 1), (1, 1), (4, 1)])],
    [(6, [(6, 1)]), (7, [(6, 1), (2, -1), (5, 1)])],
    [(7, [(7, 1)]), (6, [(4, 1)])],
]

F32, BF16 = jnp.float32, jnp.bfloat16
MESH = pl.DeviceIdType.MESH


class Tables:
    def __init__(self, plan):
        n = len(plan)
        self.n = n
        self.tasks = [[(l, z, m, t) for t, (m, ls) in enumerate(plan[p]) for l, z in ls] for p in range(n)]
        self.targets = max(len(plan[p]) for p in range(n))
        self.depth = max(len(k) for k in self.tasks)
        self.ntargets = [len(plan[p]) for p in range(n)]
        self.target = [[m for m, _ in plan[p]] for p in range(n)]
        self.start = [[min(k for k, task in enumerate(self.tasks[p]) if task[3] == t) for t in range(len(plan[p]))] for p in range(n)]
        self.stop = [[max(k for k, task in enumerate(self.tasks[p]) if task[3] == t) + 1 for t in range(len(plan[p]))] for p in range(n)]
        self.late = [[int(any(l != p for l, _ in ls)) for _, ls in plan[p]] for p in range(n)]
        self.sources = []
        for p in range(n):
            seen = []
            for l, z, _, _ in self.tasks[p]:
                if l != p and (l, z) not in seen:
                    seen.append((l, z))
            self.sources.append(seen)
        self.task_latent = [[0 if l == p else 1 + self.sources[p].index((l, z)) for l, z, _, _ in self.tasks[p]] for p in range(n)]
        self.task_new = [[int(s > 0 and s not in self.task_latent[p][:k]) for k, s in enumerate(self.task_latent[p])] for p in range(n)]
        self.task_target = [[m for _, _, m, _ in self.tasks[p]] for p in range(n)]
        self.dec = [[(p, z, m, k) for k in range(self.depth) for p in range(n) for kk, (a, z, m, _) in enumerate(self.tasks[p]) if a == l != p and kk == k] for l in range(n)]
        for l in range(n):
            self.dec[l].sort(key=lambda d: d[0] // 4 != l // 4)
        self.near = [sum(d[0] // 4 == l // 4 for d in self.dec[l]) for l in range(n)]
        self.lat = [[(p, z, 1 + s) for p in range(n) for s, (a, z) in enumerate(self.sources[p]) if a == l] for l in range(n)]
        self.adders = [[m] + [p for p in range(n) if p != m and m in self.target[p]] for m in range(n)]
        self.most_adders = max(len(a) for a in self.adders)
        self.adder_slot = [[self.adders[m].index(p) for m in self.target[p]] for p in range(n)]
        for p in range(n):
            assert p in self.target[p] and len(self.tasks[p]) <= 8


def word(values):
    total = sum(v << (4 * i) for i, v in enumerate(values))
    return total - (1 << 32) if total >= 1 << 31 else total


def pick(index, values):
    result = jnp.int32(values[0])
    for i, value in enumerate(values[1:], 1):
        result = jnp.where(index == i, jnp.int32(value), result)
    return result


def words(index, lists):
    return pick(index, [word(values) for values in lists])


def nibble(packed, i):
    return lax.bitwise_and(lax.shift_right_logical(packed, jnp.int32(4 * i)), jnp.int32(15))


def kernel(
    tab, acts, enc, enc_bias, dec, dec_bias, out,
    every, enc_v, latents, decs, acc, core_out, core_in, y_out, y_own, y_in, z_out, z_own, z_in,
    s_in, s_dec, s_task, r_task, s_lat, r_lat, s_gz, r_gz, s_gy, r_gy, s_gc, r_gc,
    s_core, r_core, s_y, r_y, s_z, r_z,
):
    me = lax.axis_index("layer")
    lat = lax.axis_index("lat")
    zh, y, c = lat // 8, (lat // 2) % 4, lat % 2
    width = acts.shape[2]

    def device(layer, zh_, y_, c_):
        return (layer, (zh_ % 4) * 8 + (y_ % 4) * 2 + c_)

    def remote(src, dst, send, recv, where):
        return pltpu.make_async_remote_copy(
            src_ref=src, dst_ref=dst, send_sem=send, recv_sem=recv, device_id=where, device_id_type=MESH
        )

    def rows(start, size):
        return pl.ds(pl.multiple_of(start, 16), size)

    n_targets = pick(me, tab.ntargets)
    n_tasks = pick(me, [len(k) for k in tab.tasks])
    w_target = words(me, tab.target)
    w_start = words(me, tab.start)
    w_stop = words(me, tab.stop)
    w_late = words(me, tab.late)
    w_task_lat = words(me, tab.task_latent)
    w_task_new = words(me, tab.task_new)
    w_task_m = words(me, tab.task_target)
    n_dec = pick(me, [len(d) for d in tab.dec])
    n_near = pick(me, tab.near)
    w_dec_p = words(me, [[d[0] for d in ds] for ds in tab.dec])
    w_dec_z = words(me, [[int(d[1] < 0) for d in ds] for ds in tab.dec])
    w_dec_m = words(me, [[d[2] for d in ds] for ds in tab.dec])
    w_dec_k = words(me, [[d[3] for d in ds] for ds in tab.dec])
    n_lat = pick(me, [len(d) for d in tab.lat])
    w_lat_p = words(me, [[d[0] for d in ds] for ds in tab.lat])
    w_lat_z = words(me, [[int(d[1] < 0) for d in ds] for ds in tab.lat])
    w_lat_s = words(me, [[d[2] for d in ds] for ds in tab.lat])
    n_src = pick(me, [len(d) for d in tab.sources])
    w_src_l = words(me, [[d[0] for d in ds] for ds in tab.sources])
    w_src_z = words(me, [[int(d[1] < 0) for d in ds] for ds in tab.sources])
    n_add = pick(me, [len(d) for d in tab.adders])
    w_add_p = words(me, tab.adders)
    w_slot = words(me, tab.adder_slot)

    own_block = c * 16 + y * 4 + zh
    in_acts = pltpu.make_async_copy(acts.at[0], every.at[rows(own_block * 16, 16)], s_in.at[0])
    in_enc = pltpu.make_async_copy(enc.at[0], enc_v, s_in.at[1])
    in_acts.start()
    in_enc.start()

    def local_dec(k):
        return pltpu.make_async_copy(dec.at[0, nibble(w_task_m, k)], decs.at[k], s_dec.at[k])

    @pl.loop(0, n_tasks)
    def _(k):
        @pl.when(nibble(w_task_lat, k) == 0)
        def _():
            local_dec(k).start()

    barrier = pltpu.get_barrier_semaphore()

    def greet(where):
        pl.semaphore_signal(barrier, inc=1, device_id=where, device_id_type=MESH)

    greet(device(me, zh, y, 1 - c))
    for step in (1, 3):
        greet(device(me, zh + step, y, c))
    for step in (1, 2, 3):
        greet(device(me, zh, y + step, c))

    @pl.loop(0, n_src)
    def _(i):
        greet(device(nibble(w_src_l, i), zh + nibble(w_src_z, i), y, c))

    @pl.loop(1, n_add)
    def _(i):
        greet(device(nibble(w_add_p, i), zh, y, c))

    in_acts.wait()
    pl.semaphore_wait(barrier, 6 + n_lat + (n_targets - 1))

    def block(from_y, from_zh):
        return every.at[rows((c * 16 + (from_y % 4) * 4 + from_zh % 4) * 16, 16)]

    def gather_z(step):
        part = block(y, zh + 3 if step == 2 else zh)
        return remote(part, part, s_gz.at[step - 1], r_gz.at[step - 1], device(me, zh + (1 if step == 2 else step), y, c))

    def gather_y(step, off):
        part = block(y, zh + off)
        return remote(part, part, s_gy.at[step - 1, off], r_gy.at[step - 1, off], device(me, zh, y + step, c))

    def gather_c(step, off):
        part = block(y + 4 - step, zh + off)
        return remote(part, part, s_gc.at[step, off], r_gc.at[step, off], device(me, zh, y, 1 - c))

    def spread(off):
        for step in (2, 1, 3):
            gather_y(step, off).start()
        gather_c(0, off).start()

    gather_z(1).start()
    gather_z(3).start()
    spread(0)

    def send_dec(j):
        k = nibble(w_dec_k, j)
        return remote(
            dec.at[0, nibble(w_dec_m, j)], decs.at[k], s_task.at[j], r_task.at[k],
            device(nibble(w_dec_p, j), zh + 4 - nibble(w_dec_z, j), y, c),
        )

    @pl.loop(0, n_near)
    def _(j):
        send_dec(j).start()

    gather_z(1).wait_recv()
    gather_z(2).start()
    spread(3)
    gather_z(3).wait_recv()
    spread(1)
    gather_z(2).wait_recv()
    spread(2)

    @pl.loop(n_near, n_dec)
    def _(j):
        send_dec(j).start()

    for off in (0, 3, 1, 2):
        for step in (1, 3, 2):
            gather_y(step, off).wait_recv()
            gather_c(step, off).start()
    in_enc.wait()

    def encode(half):
        pre = jnp.dot(every[rows(half * 256, 256), :], enc_v[...], preferred_element_type=F32) + enc_bias[...]
        latents[0, rows(half * 256, 256), :] = jnp.maximum(pre, 0.0).astype(BF16)

    def send_latent(i, part):
        half = c if part == 0 else 1 - c
        s = nibble(w_lat_s, i)
        return remote(
            latents.at[0, rows(half * 256, 256)], latents.at[s, rows(half * 256, 256)],
            s_lat.at[i, part], r_lat.at[s, part],
            device(nibble(w_lat_p, i), zh + 4 - nibble(w_lat_z, i), y, c),
        )

    encode(c)

    @pl.loop(0, n_lat)
    def _(i):
        send_latent(i, 0).start()

    for step in range(4):
        for off in range(4):
            gather_c(step, off).wait_recv()
    encode(1 - c)

    @pl.loop(0, n_lat)
    def _(i):
        send_latent(i, 1).start()

    def recv_latent(s, part):
        half = c if part == 0 else 1 - c
        block = latents.at[s, rows(half * 256, 256)]
        return remote(block, block, s_lat.at[0, part], r_lat.at[s, part], device(me, zh, y, 1 - c))

    def recv_dec(k):
        return remote(decs.at[k], decs.at[k], s_task.at[0], r_task.at[k], device(me, zh, y, 1 - c))

    def core_copy(t):
        return remote(core_out.at[t], core_in.at[t], s_core.at[t], r_core.at[t], device(me, zh, y, 1 - c))

    def y_copy(t, step):
        return remote(
            y_out.at[t, rows(((y + step) % 4) * 64, 64)], y_in.at[t, step - 1],
            s_y.at[t, step - 1], r_y.at[t, step - 1], device(me, zh, y + step, c),
        )

    def multiply(t):
        start = nibble(w_start, t)

        @pl.loop(start, nibble(w_stop, t))
        def _(k):
            s = nibble(w_task_lat, k)

            @pl.when(s == 0)
            def _():
                local_dec(k).wait()

            @pl.when(nibble(w_task_new, k) == 1)
            def _():
                recv_latent(s, 0).wait_recv()
                recv_latent(s, 1).wait_recv()

            @pl.when(s > 0)
            def _():
                recv_dec(k).wait_recv()

            @pl.loop(0, width // 256)
            def _(i):
                columns = pl.ds(pl.multiple_of(i * 256, 256), 256)
                term = jnp.dot(latents[s], decs[k, :, columns], preferred_element_type=F32)

                @pl.when(k == start)
                def _():
                    acc[t, :, columns] = term

                @pl.when(k > start)
                def _():
                    acc[t, :, columns] += term

        @pl.loop(0, 4)
        def _(i):
            core_out[t, rows(i * 64, 64), :] = acc[t, rows((1 - c) * 256 + i * 64, 64), :].astype(BF16)

        core_copy(t).start()

    def over_cores(t):
        core_copy(t).wait_recv()

        def total(i):
            return acc[t, rows(c * 256 + i * 64, 64), :] + core_in[t, rows(i * 64, 64), :].astype(F32)

        for step in (2, 1, 3):
            i = (y + step) % 4
            y_out[t, rows(i * 64, 64), :] = total(i).astype(BF16)
            y_copy(t, step).start()
        y_own[t] = total(y)

    def z_copy(t, step):
        m = nibble(w_target, t)
        to = (zh + step) % 4
        return remote(
            z_out.at[t, rows(to * 16, 16)], z_in.at[nibble(w_slot, t), zh], s_z.at[t, step],
            r_z.at[nibble(w_slot, t), zh], device(m, to, y, c),
        )

    def over_y(t):
        total = y_own[t]
        for step in (1, 3, 2):
            y_copy(t, step).wait_recv()
            total = total + y_in[t, step - 1].astype(F32)
        z_out[t] = total.astype(BF16)
        y_own[t] = total

        for step in (2, 1, 3):
            z_copy(t, step).start()

        @pl.when(nibble(w_target, t) != me)
        def _():
            z_copy(t, 0).start()

        @pl.when(nibble(w_target, t) == me)
        def _():
            z_own[...] = y_own[t, rows(zh * 16, 16), :]

    @pl.loop(0, tab.targets + 2)
    def _(i):
        late = (i < n_targets) & (nibble(w_late, i) == 1)

        @pl.when((i < n_targets) & jnp.logical_not(late))
        def _():
            multiply(i)

        @pl.when((i >= 1) & (i - 1 < n_targets))
        def _():
            over_cores(i - 1)

        @pl.when((i >= 2) & (i - 2 < n_targets))
        def _():
            over_y(i - 2)

        @pl.when(late)
        def _():
            multiply(i)

    def recv_z(a, from_zh):
        block = z_in.at[a, from_zh]
        return remote(block, block, s_z.at[0, 0], r_z.at[a, from_zh], device(me, zh, y, 1 - c))

    for step in (1, 2, 3):
        recv_z(0, (zh + step) % 4).wait_recv()
        z_own[...] += z_in[0, (zh + step) % 4].astype(F32)

    @pl.loop(1, n_add)
    def _(a):
        for step in range(4):
            recv_z(a, step).wait_recv()
            z_own[...] += z_in[a, step].astype(F32)

    out[0] = (z_own[...] + dec_bias[...]).astype(BF16)

    for step in (1, 2, 3):
        gather_z(step).wait_send()
        for off in range(4):
            gather_y(step, off).wait_send()
    for step in range(4):
        for off in range(4):
            gather_c(step, off).wait_send()

    @pl.loop(0, n_dec)
    def _(j):
        send_dec(j).wait_send()

    @pl.loop(0, n_lat)
    def _(i):
        send_latent(i, 0).wait_send()
        send_latent(i, 1).wait_send()

    @pl.loop(0, n_targets)
    def _(t):
        core_copy(t).wait_send()
        for step in (1, 2, 3):
            y_copy(t, step).wait_send()
            z_copy(t, step).wait_send()

        @pl.when(nibble(w_target, t) != me)
        def _():
            z_copy(t, 0).wait_send()


def solution(mesh):
    tab = Tables(PLAN)
    n_lat = 1 + max(len(s) for s in tab.sources)
    T, K, A = tab.targets, tab.depth, tab.most_adders
    J = max(max(len(d) for d in tab.dec), 1)
    N = max(max(len(d) for d in tab.lat), 1)
    DMA = pltpu.SemaphoreType.DMA

    def local(acts, enc_weight, enc_bias, dec_weight, dec_bias):
        width = acts.shape[2]
        return pl.pallas_call(
            functools.partial(kernel, tab),
            out_shape=jax.ShapeDtypeStruct((1, 16, width), BF16),
            in_specs=[
                pl.BlockSpec(memory_space=pl.ANY),
                pl.BlockSpec(memory_space=pl.ANY),
                pl.BlockSpec(memory_space=pltpu.VMEM),
                pl.BlockSpec(memory_space=pl.ANY),
                pl.BlockSpec(memory_space=pltpu.VMEM),
            ],
            out_specs=pl.BlockSpec(memory_space=pltpu.VMEM),
            scratch_shapes=[
                pltpu.VMEM((512, width), BF16),
                pltpu.VMEM((width, 256), BF16),
                pltpu.VMEM((n_lat, 512, 256), BF16),
                pltpu.VMEM((K, 256, width), BF16),
                pltpu.VMEM((T, 512, width), F32),
                pltpu.VMEM((T, 256, width), BF16),
                pltpu.VMEM((T, 256, width), BF16),
                pltpu.VMEM((T, 256, width), BF16),
                pltpu.VMEM((T, 64, width), F32),
                pltpu.VMEM((T, 3, 64, width), BF16),
                pltpu.VMEM((T, 64, width), BF16),
                pltpu.VMEM((16, width), F32),
                pltpu.VMEM((A, 4, 16, width), BF16),
                DMA((2,)),
                DMA((K,)),
                DMA((J,)),
                DMA((K,)),
                DMA((N, 2)),
                DMA((n_lat, 2)),
                DMA((3,)),
                DMA((3,)),
                DMA((3, 4)),
                DMA((3, 4)),
                DMA((4, 4)),
                DMA((4, 4)),
                DMA((T,)),
                DMA((T,)),
                DMA((T, 3)),
                DMA((T, 3)),
                DMA((T, 4)),
                DMA((A, 4)),
            ],
            compiler_params=pltpu.CompilerParams(
                collective_id=0, has_side_effects=True, vmem_limit_bytes=60 * 2**20
            ),
        )(acts, enc_weight, enc_bias, dec_weight, dec_bias)

    return jax.shard_map(
        local,
        mesh=mesh,
        in_specs=(
            P("layer", "lat", None),
            P("layer", None, "lat"),
            P("layer", "lat"),
            P("layer", None, "lat", None),
            P("layer", None),
        ),
        out_specs=P("layer", "lat", None),
        check_vma=False,
    )
```

```python
import functools

import jax
import jax.numpy as jnp
from jax import lax
from jax.experimental import pallas as pl
from jax.experimental.pallas import tpu as pltpu
from jax.sharding import PartitionSpec as P

PLAN = [
    [(1, [(0, 1)]), (3, [(0, 1)]), (0, [(0, 1)]), (2, [(0, 1), (1, 1)])],
    [(4, [(1, 1)]), (7, [(1, 1)]), (1, [(1, 1)]), (6, [(1, 1), (0, 1)])],
    [(4, [(2, 1)]), (2, [(2, 1)]), (3, [(2, 1), (1, 1)]), (6, [(2, 1), (3, 1)])],
    [(4, [(3, 1)]), (7, [(3, 1)]), (3, [(3, 1)]), (5, [(3, 1), (0, 1), (2, 1)])],
    [(7, [(4, 1), (0, 1)]), (4, [(4, 1), (0, -1)])],
    [(6, [(5, 1)]), (5, [(5, 1), (1, 1), (4, 1)])],
    [(6, [(6, 1)]), (7, [(6, 1), (2, -1), (5, 1)])],
    [(7, [(7, 1)]), (6, [(4, 1)])],
]

F32, BF16 = jnp.float32, jnp.bfloat16
MESH = pl.DeviceIdType.MESH


PIECES = 1


class Tables:
    def __init__(self, plan):
        n = len(plan)
        layers = range(n)
        self.tasks = [[(l, z, q, t) for t, (q, ls) in enumerate(plan[p]) for l, z in ls] for p in layers]
        self.slots = max(len(plan[p]) for p in layers)
        self.depth = max(len(k) for k in self.tasks)
        self.nslots = [len(plan[p]) for p in layers]
        self.piece = [[q for q, _ in plan[p]] for p in layers]
        self.start = [[min(k for k, task in enumerate(self.tasks[p]) if task[3] == t) for t in range(len(plan[p]))] for p in layers]
        self.stop = [[max(k for k, task in enumerate(self.tasks[p]) if task[3] == t) + 1 for t in range(len(plan[p]))] for p in layers]
        self.late = [[int(any(l != p for l, _ in ls)) for _, ls in plan[p]] for p in layers]
        self.sources = []
        for p in layers:
            seen = []
            for l, z, _, _ in self.tasks[p]:
                if l != p and (l, z) not in seen:
                    seen.append((l, z))
            self.sources.append(seen)
        self.task_latent = [[0 if l == p else 1 + self.sources[p].index((l, z)) for l, z, _, _ in self.tasks[p]] for p in layers]
        self.task_new = [[int(s > 0 and s not in self.task_latent[p][:k]) for k, s in enumerate(self.task_latent[p])] for p in layers]
        self.task_piece = [[q for _, _, q, _ in self.tasks[p]] for p in layers]
        self.dec = [[(p, z, q, k) for k in range(self.depth) for p in layers for kk, (a, z, q, _) in enumerate(self.tasks[p]) if a == l != p and kk == k] for l in layers]
        for l in layers:
            self.dec[l].sort(key=lambda d: d[0] // 4 != l // 4)
        self.near = [sum(d[0] // 4 == l // 4 for d in self.dec[l]) for l in layers]
        self.lat = [[(p, z, 1 + s) for p in layers for s, (a, z) in enumerate(self.sources[p]) if a == l] for l in layers]
        self.adders = [[q // PIECES] + [p for p in layers if p != q // PIECES and q in self.piece[p]] for q in range(n * PIECES)]
        self.most_adders = max(len(a) for a in self.adders)
        self.adder_place = [[self.adders[q].index(p) for q in self.piece[p]] for p in layers]
        self.adds_to = [[m for m in layers if m != p and any(q // PIECES == m for q in self.piece[p])] for p in layers]
        self.added_by = [[p for p in layers if m in self.adds_to[p]] for m in layers]
        for p in layers:
            assert all(p * PIECES + h in self.piece[p] for h in range(PIECES)) and len(self.tasks[p]) <= 16


def word(values):
    total = sum(v << (4 * i) for i, v in enumerate(values))
    return total - (1 << 32) if total >= 1 << 31 else total


def pick(index, values):
    result = jnp.int32(values[0])
    for i, value in enumerate(values[1:], 1):
        result = jnp.where(index == i, jnp.int32(value), result)
    return result


def words(index, lists):
    low = pick(index, [word(values[:8]) for values in lists])
    high = pick(index, [word(values[8:]) for values in lists])
    return low, high


def nibble(packed, i):
    low, high = packed
    chosen = jnp.where(i < 8, low, high)
    return lax.bitwise_and(lax.shift_right_logical(chosen, jnp.int32(4 * (i % 8))), jnp.int32(15))


def kernel(
    tab, acts, enc, enc_bias, dec, dec_bias, out,
    every, enc_v, latents, decs, acc, core_out, core_in, y_out, y_half, y_own, y_in, z_out, z_own, z_in,
    s_in, s_dec, s_task, r_task, s_lat, r_lat, s_gz, r_gz, s_gy, r_gy, s_gc, r_gc,
    s_core, r_core, s_y, r_y, s_z, r_z,
):
    me = lax.axis_index("layer")
    lat = lax.axis_index("lat")
    zh, y, c = lat // 8, (lat // 2) % 4, lat % 2
    width = acts.shape[2] // PIECES

    def device(layer, zh_, y_, c_):
        return (layer, (zh_ % 4) * 8 + (y_ % 4) * 2 + c_)

    def remote(src, dst, send, recv, where):
        return pltpu.make_async_remote_copy(
            src_ref=src, dst_ref=dst, send_sem=send, recv_sem=recv, device_id=where, device_id_type=MESH
        )

    def rows(start, size):
        return pl.ds(pl.multiple_of(start, 16), size)

    n_slots = pick(me, tab.nslots)
    n_tasks = pick(me, [len(k) for k in tab.tasks])
    w_piece = words(me, tab.piece)
    w_start = words(me, tab.start)
    w_stop = words(me, tab.stop)
    w_late = words(me, tab.late)
    w_task_lat = words(me, tab.task_latent)
    w_task_new = words(me, tab.task_new)
    w_task_q = words(me, tab.task_piece)
    n_dec = pick(me, [len(d) for d in tab.dec])
    n_near = pick(me, tab.near)
    w_dec_p = words(me, [[d[0] for d in ds] for ds in tab.dec])
    w_dec_z = words(me, [[int(d[1] < 0) for d in ds] for ds in tab.dec])
    w_dec_q = words(me, [[d[2] for d in ds] for ds in tab.dec])
    w_dec_k = words(me, [[d[3] for d in ds] for ds in tab.dec])
    n_lat = pick(me, [len(d) for d in tab.lat])
    w_lat_p = words(me, [[d[0] for d in ds] for ds in tab.lat])
    w_lat_z = words(me, [[int(d[1] < 0) for d in ds] for ds in tab.lat])
    w_lat_s = words(me, [[d[2] for d in ds] for ds in tab.lat])
    n_src = pick(me, [len(d) for d in tab.sources])
    w_src_l = words(me, [[d[0] for d in ds] for ds in tab.sources])
    w_src_z = words(me, [[int(d[1] < 0) for d in ds] for ds in tab.sources])
    n_to = pick(me, [len(d) for d in tab.adds_to])
    n_by = pick(me, [len(d) for d in tab.added_by])
    w_by = words(me, tab.added_by)
    w_place = words(me, tab.adder_place)

    def columns(q):
        return pl.ds(pl.multiple_of((q % PIECES) * width, 128), width)

    def dec_of(q):
        return dec.at[0, q // PIECES, :, columns(q)]

    own_block = c * 16 + y * 4 + zh
    in_acts = pltpu.make_async_copy(acts.at[0], every.at[rows(own_block * 16, 16)], s_in.at[0])
    in_enc = pltpu.make_async_copy(enc.at[0], enc_v, s_in.at[1])
    in_acts.start()
    in_enc.start()

    def local_dec(k):
        return pltpu.make_async_copy(dec_of(nibble(w_task_q, k)), decs.at[k], s_dec.at[k])

    @pl.loop(0, n_tasks)
    def _(k):
        @pl.when(nibble(w_task_lat, k) == 0)
        def _():
            local_dec(k).start()

    barrier = pltpu.get_barrier_semaphore()

    def greet(where):
        pl.semaphore_signal(barrier, inc=1, device_id=where, device_id_type=MESH)

    greet(device(me, zh, y, 1 - c))
    for step in (1, 3):
        greet(device(me, zh + step, y, c))
    for step in (1, 2, 3):
        greet(device(me, zh, y + step, c))

    @pl.loop(0, n_src)
    def _(i):
        greet(device(nibble(w_src_l, i), zh + nibble(w_src_z, i), y, c))

    @pl.loop(0, n_by)
    def _(i):
        greet(device(nibble(w_by, i), zh, y, c))

    in_acts.wait()
    pl.semaphore_wait(barrier, 6 + n_lat + n_to)

    def block(from_y, from_zh):
        return every.at[rows((c * 16 + (from_y % 4) * 4 + from_zh % 4) * 16, 16)]

    def gather_z(step):
        part = block(y, zh + 3 if step == 2 else zh)
        return remote(part, part, s_gz.at[step - 1], r_gz.at[step - 1], device(me, zh + (1 if step == 2 else step), y, c))

    def gather_y(step, off):
        part = block(y, zh + off)
        return remote(part, part, s_gy.at[step - 1, off], r_gy.at[step - 1, off], device(me, zh, y + step, c))

    def gather_c(step, off):
        part = block(y + 4 - step, zh + off)
        return remote(part, part, s_gc.at[step, off], r_gc.at[step, off], device(me, zh, y, 1 - c))

    def spread(off):
        for step in (2, 1, 3):
            gather_y(step, off).start()
        gather_c(0, off).start()

    gather_z(1).start()
    gather_z(3).start()
    spread(0)

    def send_dec(j):
        k = nibble(w_dec_k, j)
        return remote(
            dec_of(nibble(w_dec_q, j)), decs.at[k], s_task.at[j], r_task.at[k],
            device(nibble(w_dec_p, j), zh + 4 - nibble(w_dec_z, j), y, c),
        )

    @pl.loop(0, n_near)
    def _(j):
        send_dec(j).start()

    gather_z(1).wait_recv()
    gather_z(2).start()
    spread(3)
    gather_z(3).wait_recv()
    spread(1)
    gather_z(2).wait_recv()
    spread(2)

    @pl.loop(n_near, n_dec)
    def _(j):
        send_dec(j).start()

    for off in (0, 3, 1, 2):
        for step in (1, 3, 2):
            gather_y(step, off).wait_recv()
            gather_c(step, off).start()
    in_enc.wait()

    def encode(half):
        pre = jnp.dot(every[rows(half * 256, 256), :], enc_v[...], preferred_element_type=F32) + enc_bias[...]
        latents[0, rows(half * 256, 256), :] = jnp.maximum(pre, 0.0).astype(BF16)

    def send_latent(i, part):
        half = c if part == 0 else 1 - c
        s = nibble(w_lat_s, i)
        return remote(
            latents.at[0, rows(half * 256, 256)], latents.at[s, rows(half * 256, 256)],
            s_lat.at[i, part], r_lat.at[s, part],
            device(nibble(w_lat_p, i), zh + 4 - nibble(w_lat_z, i), y, c),
        )

    encode(c)

    @pl.loop(0, n_lat)
    def _(i):
        send_latent(i, 0).start()

    for step in range(4):
        for off in range(4):
            gather_c(step, off).wait_recv()
    encode(1 - c)

    @pl.loop(0, n_lat)
    def _(i):
        send_latent(i, 1).start()

    def recv_latent(s, part):
        half = c if part == 0 else 1 - c
        block = latents.at[s, rows(half * 256, 256)]
        return remote(block, block, s_lat.at[0, part], r_lat.at[s, part], device(me, zh, y, 1 - c))

    def recv_dec(k):
        return remote(decs.at[k], decs.at[k], s_task.at[0], r_task.at[k], device(me, zh, y, 1 - c))

    def core_copy(t):
        return remote(core_out.at[t], core_in.at[t], s_core.at[t], r_core.at[t], device(me, zh, y, 1 - c))

    LEAPS = ((2, 0, 1, 0), (2, 32, 3, 1), (1, 32, 1, 2), (3, 0, 3, 3), (1, 0, 1, 4), (3, 32, 3, 5))

    def y_copy(t, leap):
        off, row, step, sem = LEAPS[leap]
        place = 0 if step == 1 else 1
        dst = y_half.at[t, place] if leap < 2 else y_in.at[t, place, pl.ds(row, 32)]
        return remote(
            y_out.at[t, rows(((y + off) % 4) * 64 + row, 32)], dst,
            s_y.at[t, sem], r_y.at[t, sem], device(me, zh, y + step, c),
        )

    def multiply(t):
        start, stop = nibble(w_start, t), nibble(w_stop, t)

        @pl.loop(start, stop)
        def _(k):
            s = nibble(w_task_lat, k)

            @pl.when(s == 0)
            def _():
                local_dec(k).wait()

            @pl.when(nibble(w_task_new, k) == 1)
            def _():
                recv_latent(s, 0).wait_recv()
                recv_latent(s, 1).wait_recv()

            @pl.when(s > 0)
            def _():
                recv_dec(k).wait_recv()

        @pl.loop(0, 2)
        def _(part):
            half = rows((c + 1 + part) % 2 * 256, 256)

            @pl.loop(start, stop)
            def _(k):
                s = nibble(w_task_lat, k)
                term = jnp.dot(latents[s, half, :], decs[k], preferred_element_type=F32)

                @pl.when(k == start)
                def _():
                    acc[t, half, :] = term

                @pl.when(k > start)
                def _():
                    acc[t, half, :] += term

            @pl.when(part == 0)
            def _():
                @pl.loop(0, 4)
                def _(i):
                    core_out[t, rows(i * 64, 64), :] = acc[t, rows((1 - c) * 256 + i * 64, 64), :].astype(BF16)

                core_copy(t).start()

    def core_total(t, off, row, size):
        i = (y + off) % 4 * 64 + row
        return acc[t, rows(c * 256 + i, size), :] + core_in[t, rows(i, size), :].astype(F32)

    def over_cores(t):
        core_copy(t).wait_recv()
        for leap in (0, 1, 2, 3):
            off, row, _, _ = LEAPS[leap]
            y_out[t, rows((y + off) % 4 * 64 + row, 32), :] = core_total(t, off, row, 32).astype(BF16)
            y_copy(t, leap).start()
        y_own[t] = core_total(t, 0, 0, 64)

    def over_half(t):
        for leap in (4, 5):
            off, row, _, _ = LEAPS[leap]
            y_copy(t, leap - 4).wait_recv()
            total = core_total(t, off, row, 32) + y_half[t, leap - 4].astype(F32)
            y_out[t, rows((y + off) % 4 * 64 + row, 32), :] = total.astype(BF16)
            y_copy(t, leap).start()

    def z_copy(t, step):
        q = nibble(w_piece, t)
        to = (zh + step) % 4
        place = nibble(w_place, t)
        return remote(
            z_out.at[t, rows(to * 16, 16)], z_in.at[q % PIECES, place, zh], s_z.at[t, step],
            r_z.at[q % PIECES, place, zh], device(q // PIECES, to, y, c),
        )

    def over_y(t):
        for leap in (2, 3, 4, 5):
            y_copy(t, leap).wait_recv()
        total = y_own[t] + y_in[t, 0].astype(F32) + y_in[t, 1].astype(F32)
        z_out[t] = total.astype(BF16)
        y_own[t] = total
        for step in (2, 1, 3):
            z_copy(t, step).start()
        q = nibble(w_piece, t)

        @pl.when(q // PIECES != me)
        def _():
            z_copy(t, 0).start()

        @pl.when(q // PIECES == me)
        def _():
            z_own[q % PIECES] = y_own[t, rows(zh * 16, 16), :]

    @pl.loop(0, tab.slots + 3)
    def _(i):
        late = (i < n_slots) & (nibble(w_late, i) == 1)
        before = (i >= 1) & (i - 1 < n_slots) & (nibble(w_late, jnp.maximum(i - 1, 0)) == 1)

        @pl.when((i < n_slots) & jnp.logical_not(late))
        def _():
            multiply(i)

        @pl.when((i >= 1) & (i - 1 < n_slots))
        def _():
            over_cores(i - 1)

        @pl.when((i >= 2) & (i - 2 < n_slots) & jnp.logical_not(before))
        def _():
            over_half(i - 2)

        @pl.when((i >= 1) & late)
        def _():
            over_half(i - 1)

        @pl.when((i >= 3) & (i - 3 < n_slots))
        def _():
            over_y(i - 3)

        @pl.when(late)
        def _():
            multiply(i)

    def recv_z(h, a, from_zh):
        got = z_in.at[h, a, from_zh]
        return remote(got, got, s_z.at[0, 0], r_z.at[h, a, from_zh], device(me, zh, y, 1 - c))

    for h in range(PIECES):
        for step in (1, 2, 3):
            recv_z(h, 0, (zh + step) % 4).wait_recv()
            z_own[h] += z_in[h, 0, (zh + step) % 4].astype(F32)

        @pl.loop(1, pick(me, [len(tab.adders[m * PIECES + h]) for m in range(len(tab.nslots))]))
        def _(a):
            for step in range(4):
                recv_z(h, a, step).wait_recv()
                z_own[h] += z_in[h, a, step].astype(F32)

        part = slice(h * width, (h + 1) * width)
        out[0, :, part] = (z_own[h] + dec_bias[:, part]).astype(BF16)

    for step in (1, 2, 3):
        gather_z(step).wait_send()
        for off in range(4):
            gather_y(step, off).wait_send()
    for step in range(4):
        for off in range(4):
            gather_c(step, off).wait_send()

    @pl.loop(0, n_dec)
    def _(j):
        send_dec(j).wait_send()

    @pl.loop(0, n_lat)
    def _(i):
        send_latent(i, 0).wait_send()
        send_latent(i, 1).wait_send()

    @pl.loop(0, n_slots)
    def _(t):
        core_copy(t).wait_send()
        for leap in range(6):
            y_copy(t, leap).wait_send()
        for step in (1, 2, 3):
            z_copy(t, step).wait_send()

        @pl.when(nibble(w_piece, t) // PIECES != me)
        def _():
            z_copy(t, 0).wait_send()


def solution(mesh):
    tab = Tables(PLAN)
    n_lat = 1 + max(len(s) for s in tab.sources)
    T, K, A = tab.slots, tab.depth, tab.most_adders
    J = max(max(len(d) for d in tab.dec), 1)
    N = max(max(len(d) for d in tab.lat), 1)
    DMA = pltpu.SemaphoreType.DMA

    def local(acts, enc_weight, enc_bias, dec_weight, dec_bias):
        whole = acts.shape[2]
        width = whole // PIECES
        return pl.pallas_call(
            functools.partial(kernel, tab),
            out_shape=jax.ShapeDtypeStruct((1, 16, whole), BF16),
            in_specs=[
                pl.BlockSpec(memory_space=pl.ANY),
                pl.BlockSpec(memory_space=pl.ANY),
                pl.BlockSpec(memory_space=pltpu.VMEM),
                pl.BlockSpec(memory_space=pl.ANY),
                pl.BlockSpec(memory_space=pltpu.VMEM),
            ],
            out_specs=pl.BlockSpec(memory_space=pltpu.VMEM),
            scratch_shapes=[
                pltpu.VMEM((512, whole), BF16),
                pltpu.VMEM((whole, 256), BF16),
                pltpu.VMEM((n_lat, 512, 256), BF16),
                pltpu.VMEM((K, 256, width), BF16),
                pltpu.VMEM((T, 512, width), F32),
                pltpu.VMEM((T, 256, width), BF16),
                pltpu.VMEM((T, 256, width), BF16),
                pltpu.VMEM((T, 256, width), BF16),
                pltpu.VMEM((T, 2, 32, width), BF16),
                pltpu.VMEM((T, 64, width), F32),
                pltpu.VMEM((T, 2, 64, width), BF16),
                pltpu.VMEM((T, 64, width), BF16),
                pltpu.VMEM((PIECES, 16, width), F32),
                pltpu.VMEM((PIECES, A, 4, 16, width), BF16),
                DMA((2,)),
                DMA((K,)),
                DMA((J,)),
                DMA((K,)),
                DMA((N, 2)),
                DMA((n_lat, 2)),
                DMA((3,)),
                DMA((3,)),
                DMA((3, 4)),
                DMA((3, 4)),
                DMA((4, 4)),
                DMA((4, 4)),
                DMA((T,)),
                DMA((T,)),
                DMA((T, 6)),
                DMA((T, 6)),
                DMA((T, 4)),
                DMA((PIECES, A, 4)),
            ],
            compiler_params=pltpu.CompilerParams(
                collective_id=0, has_side_effects=True, vmem_limit_bytes=60 * 2**20
            ),
        )(acts, enc_weight, enc_bias, dec_weight, dec_bias)

    return jax.shard_map(
        local,
        mesh=mesh,
        in_specs=(
            P("layer", "lat", None),
            P("layer", None, "lat"),
            P("layer", "lat"),
            P("layer", None, "lat", None),
            P("layer", None),
        ),
        out_specs=P("layer", "lat", None),
        check_vma=False,
    )
```

```python
import functools

import jax
import jax.numpy as jnp
from jax import lax
from jax.experimental import pallas as pl
from jax.experimental.pallas import tpu as pltpu
from jax.sharding import PartitionSpec as P

PLAN = [
    [(1, [(0, 1)]), (0, [(0, 1)]), (3, [(0, 1), (1, 1)]), (7, [(0, 1), (3, 1)])],
    [(1, [(1, 1)]), (2, [(1, 1), (0, 1)]), (7, [(1, 1), (2, 1)])],
    [(4, [(2, 1)]), (2, [(2, 1)]), (5, [(2, 1), (1, 1)])],
    [(6, [(3, 1)]), (5, [(3, 1), (0, 1)]), (3, [(3, 1), (2, 1)])],
    [(5, [(4, 1)]), (6, [(4, 1)]), (4, [(4, 1), (0, -1), (1, -1), (3, -1)])],
    [(7, [(5, 1)]), (5, [(5, 1)]), (6, [(5, 1), (1, 1), (0, 1), (2, 1)])],
    [(6, [(6, 1)])],
    [(7, [(7, 1), (4, 1), (6, 1)])],
]
ORDER = [
    [0, 1, 16, 17, 32, 2, 3, 18, 33, 19, 48, 34, 49, 35, 50, 51],
    [0, 16, 32, 1, 2, 17, 48, 18, 33, 34, 49, 50],
    [0, 1, 16, 17, 32, 2, 33, 18, 48, 49, 34, 50],
    [0, 16, 32, 1, 2, 17, 48, 18, 33, 34, 49, 50],
    [0, 1, 16, 17, 32, 33, 48, 2, 49, 18, 34, 50],
    [0, 1, 16, 17, 32, 33, 48, 2, 49, 18, 34, 50],
    [0, 16, 32, 48],
    [0, 16, 32, 48],
]

F32, BF16 = jnp.float32, jnp.bfloat16
MESH = pl.DeviceIdType.MESH


PIECES = 1


class Tables:
    def __init__(self, plan):
        n = len(plan)
        layers = range(n)
        self.tasks = [[(l, z, q, t) for t, (q, ls) in enumerate(plan[p]) for l, z in ls] for p in layers]
        self.slots = max(len(plan[p]) for p in layers)
        self.depth = max(len(k) for k in self.tasks)
        self.nslots = [len(plan[p]) for p in layers]
        self.piece = [[q for q, _ in plan[p]] for p in layers]
        self.start = [[min(k for k, task in enumerate(self.tasks[p]) if task[3] == t) for t in range(len(plan[p]))] for p in layers]
        self.stop = [[max(k for k, task in enumerate(self.tasks[p]) if task[3] == t) + 1 for t in range(len(plan[p]))] for p in layers]
        self.sources = []
        for p in layers:
            seen = []
            for l, z, _, _ in self.tasks[p]:
                if l != p and (l, z) not in seen:
                    seen.append((l, z))
            self.sources.append(seen)
        self.task_latent = [[0 if l == p else 1 + self.sources[p].index((l, z)) for l, z, _, _ in self.tasks[p]] for p in layers]
        self.task_new = [[int(s > 0 and s not in self.task_latent[p][:k]) for k, s in enumerate(self.task_latent[p])] for p in layers]
        self.task_piece = [[q for _, _, q, _ in self.tasks[p]] for p in layers]
        self.dec = [[(p, z, q, k) for k in range(self.depth) for p in layers for kk, (a, z, q, _) in enumerate(self.tasks[p]) if a == l != p and kk == k] for l in layers]
        for l in layers:
            self.dec[l].sort(key=lambda d: d[0] // 4 != l // 4)
        self.near = [sum(d[0] // 4 == l // 4 for d in self.dec[l]) for l in layers]
        self.lat = [[(p, z, 1 + s) for p in layers for s, (a, z) in enumerate(self.sources[p]) if a == l] for l in layers]
        self.adders = [[q // PIECES] + [p for p in layers if p != q // PIECES and q in self.piece[p]] for q in range(n * PIECES)]
        self.most_adders = max(len(a) for a in self.adders)
        self.adder_place = [[self.adders[q].index(p) for q in self.piece[p]] for p in layers]
        self.adds_to = [[m for m in layers if m != p and any(q // PIECES == m for q in self.piece[p])] for p in layers]
        self.added_by = [[p for p in layers if m in self.adds_to[p]] for m in layers]
        for p in layers:
            assert all(p * PIECES + h in self.piece[p] for h in range(PIECES)) and len(self.tasks[p]) <= 16


def word(values):
    total = sum(v << (4 * i) for i, v in enumerate(values))
    return total - (1 << 32) if total >= 1 << 31 else total


def pick(index, values):
    result = jnp.int32(values[0])
    for i, value in enumerate(values[1:], 1):
        result = jnp.where(index == i, jnp.int32(value), result)
    return result


def words(index, lists):
    most = max(len(values) for values in lists)
    return [pick(index, [word(values[at : at + 8]) for values in lists]) for at in range(0, max(most, 1), 8)]


def nibble(packed, i):
    chosen = packed[0]
    for at, other in enumerate(packed[1:], 1):
        chosen = jnp.where(i >= 8 * at, other, chosen)
    return lax.bitwise_and(lax.shift_right_logical(chosen, jnp.int32(4 * (i % 8))), jnp.int32(15))


def kernel(
    tab, acts, enc, enc_bias, dec, dec_bias, out,
    every, enc_v, latents, decs, acc, core_out, core_in, y_out, y_half, y_own, y_in, z_out, z_own, z_in,
    s_in, s_dec, s_task, r_task, s_lat, r_lat, s_gz, r_gz, s_gy, r_gy, s_gc, r_gc,
    s_core, r_core, s_y, r_y, s_z, r_z,
):
    me = lax.axis_index("layer")
    lat = lax.axis_index("lat")
    zh, y, c = lat // 8, (lat // 2) % 4, lat % 2
    width = acts.shape[2] // PIECES

    def device(layer, zh_, y_, c_):
        return (layer, (zh_ % 4) * 8 + (y_ % 4) * 2 + c_)

    def remote(src, dst, send, recv, where):
        return pltpu.make_async_remote_copy(
            src_ref=src, dst_ref=dst, send_sem=send, recv_sem=recv, device_id=where, device_id_type=MESH
        )

    def rows(start, size):
        return pl.ds(pl.multiple_of(start, 16), size)

    n_slots = pick(me, tab.nslots)
    n_tasks = pick(me, [len(k) for k in tab.tasks])
    w_piece = words(me, tab.piece)
    w_start = words(me, tab.start)
    w_stop = words(me, tab.stop)
    n_steps = pick(me, [len(o) for o in ORDER])
    w_kind = words(me, [[v // 16 for v in o] for o in ORDER])
    w_step = words(me, [[v % 16 for v in o] for o in ORDER])
    w_task_lat = words(me, tab.task_latent)
    w_task_new = words(me, tab.task_new)
    w_task_q = words(me, tab.task_piece)
    n_dec = pick(me, [len(d) for d in tab.dec])
    n_near = pick(me, tab.near)
    w_dec_p = words(me, [[d[0] for d in ds] for ds in tab.dec])
    w_dec_z = words(me, [[int(d[1] < 0) for d in ds] for ds in tab.dec])
    w_dec_q = words(me, [[d[2] for d in ds] for ds in tab.dec])
    w_dec_k = words(me, [[d[3] for d in ds] for ds in tab.dec])
    n_lat = pick(me, [len(d) for d in tab.lat])
    w_lat_p = words(me, [[d[0] for d in ds] for ds in tab.lat])
    w_lat_z = words(me, [[int(d[1] < 0) for d in ds] for ds in tab.lat])
    w_lat_s = words(me, [[d[2] for d in ds] for ds in tab.lat])
    n_src = pick(me, [len(d) for d in tab.sources])
    w_src_l = words(me, [[d[0] for d in ds] for ds in tab.sources])
    w_src_z = words(me, [[int(d[1] < 0) for d in ds] for ds in tab.sources])
    n_to = pick(me, [len(d) for d in tab.adds_to])
    n_by = pick(me, [len(d) for d in tab.added_by])
    w_by = words(me, tab.added_by)
    w_place = words(me, tab.adder_place)

    def columns(q):
        return pl.ds(pl.multiple_of((q % PIECES) * width, 128), width)

    def dec_of(q):
        return dec.at[0, q // PIECES, :, columns(q)]

    own_block = c * 16 + y * 4 + zh
    in_acts = pltpu.make_async_copy(acts.at[0], every.at[rows(own_block * 16, 16)], s_in.at[0])
    in_enc = pltpu.make_async_copy(enc.at[0], enc_v, s_in.at[1])
    in_acts.start()
    in_enc.start()

    def local_dec(k):
        return pltpu.make_async_copy(dec_of(nibble(w_task_q, k)), decs.at[k], s_dec.at[k])

    @pl.loop(0, n_tasks)
    def _(k):
        @pl.when(nibble(w_task_lat, k) == 0)
        def _():
            local_dec(k).start()

    barrier = pltpu.get_barrier_semaphore()

    def greet(where):
        pl.semaphore_signal(barrier, inc=1, device_id=where, device_id_type=MESH)

    greet(device(me, zh, y, 1 - c))
    for step in (1, 3):
        greet(device(me, zh + step, y, c))
    for step in (1, 2, 3):
        greet(device(me, zh, y + step, c))

    @pl.loop(0, n_src)
    def _(i):
        greet(device(nibble(w_src_l, i), zh + nibble(w_src_z, i), y, c))

    @pl.loop(0, n_by)
    def _(i):
        greet(device(nibble(w_by, i), zh, y, c))

    in_acts.wait()
    pl.semaphore_wait(barrier, 6 + n_lat + n_to)

    def block(from_y, from_zh):
        return every.at[rows((c * 16 + (from_y % 4) * 4 + from_zh % 4) * 16, 16)]

    def gather_z(step):
        part = block(y, zh + 3 if step == 2 else zh)
        return remote(part, part, s_gz.at[step - 1], r_gz.at[step - 1], device(me, zh + (1 if step == 2 else step), y, c))

    def gather_y(step, off):
        part = block(y, zh + off)
        return remote(part, part, s_gy.at[step - 1, off], r_gy.at[step - 1, off], device(me, zh, y + step, c))

    def gather_c(step, off):
        part = block(y + 4 - step, zh + off)
        return remote(part, part, s_gc.at[step, off], r_gc.at[step, off], device(me, zh, y, 1 - c))

    def spread(off):
        for step in (2, 1, 3):
            gather_y(step, off).start()
        gather_c(0, off).start()

    gather_z(1).start()
    gather_z(3).start()
    spread(0)

    def send_dec(j):
        k = nibble(w_dec_k, j)
        return remote(
            dec_of(nibble(w_dec_q, j)), decs.at[k], s_task.at[j], r_task.at[k],
            device(nibble(w_dec_p, j), zh + 4 - nibble(w_dec_z, j), y, c),
        )

    @pl.loop(0, n_near)
    def _(j):
        send_dec(j).start()

    gather_z(1).wait_recv()
    gather_z(2).start()
    spread(3)
    gather_z(3).wait_recv()
    spread(1)
    gather_z(2).wait_recv()
    spread(2)

    @pl.loop(n_near, n_dec)
    def _(j):
        send_dec(j).start()

    for off in (0, 3, 1, 2):
        for step in (1, 3, 2):
            gather_y(step, off).wait_recv()
            gather_c(step, off).start()
    in_enc.wait()

    def encode(half):
        pre = jnp.dot(every[rows(half * 256, 256), :], enc_v[...], preferred_element_type=F32) + enc_bias[...]
        latents[0, rows(half * 256, 256), :] = jnp.maximum(pre, 0.0).astype(BF16)

    def send_latent(i, part):
        half = c if part == 0 else 1 - c
        s = nibble(w_lat_s, i)
        return remote(
            latents.at[0, rows(half * 256, 256)], latents.at[s, rows(half * 256, 256)],
            s_lat.at[i, part], r_lat.at[s, part],
            device(nibble(w_lat_p, i), zh + 4 - nibble(w_lat_z, i), y, c),
        )

    encode(c)

    @pl.loop(0, n_lat)
    def _(i):
        send_latent(i, 0).start()

    for step in range(4):
        for off in range(4):
            gather_c(step, off).wait_recv()
    encode(1 - c)

    @pl.loop(0, n_lat)
    def _(i):
        send_latent(i, 1).start()

    def recv_latent(s, part):
        half = c if part == 0 else 1 - c
        block = latents.at[s, rows(half * 256, 256)]
        return remote(block, block, s_lat.at[0, part], r_lat.at[s, part], device(me, zh, y, 1 - c))

    def recv_dec(k):
        return remote(decs.at[k], decs.at[k], s_task.at[0], r_task.at[k], device(me, zh, y, 1 - c))

    def core_copy(t):
        return remote(core_out.at[t], core_in.at[t], s_core.at[t], r_core.at[t], device(me, zh, y, 1 - c))

    LEAPS = ((2, 0, 1, 0), (2, 32, 3, 1), (1, 32, 1, 2), (3, 0, 3, 3), (1, 0, 1, 4), (3, 32, 3, 5))

    def y_copy(t, leap):
        off, row, step, sem = LEAPS[leap]
        place = 0 if step == 1 else 1
        dst = y_half.at[t, place] if leap < 2 else y_in.at[t, place, pl.ds(row, 32)]
        return remote(
            y_out.at[t, rows(((y + off) % 4) * 64 + row, 32)], dst,
            s_y.at[t, sem], r_y.at[t, sem], device(me, zh, y + step, c),
        )

    def multiply(t):
        start, stop = nibble(w_start, t), nibble(w_stop, t)

        @pl.loop(start, stop)
        def _(k):
            s = nibble(w_task_lat, k)

            @pl.when(s == 0)
            def _():
                local_dec(k).wait()

            @pl.when(nibble(w_task_new, k) == 1)
            def _():
                recv_latent(s, 0).wait_recv()
                recv_latent(s, 1).wait_recv()

            @pl.when(s > 0)
            def _():
                recv_dec(k).wait_recv()

        @pl.loop(0, 2)
        def _(part):
            half = rows((c + 1 + part) % 2 * 256, 256)

            @pl.loop(start, stop)
            def _(k):
                s = nibble(w_task_lat, k)
                term = jnp.dot(latents[s, half, :], decs[k], preferred_element_type=F32)

                @pl.when(k == start)
                def _():
                    acc[t, half, :] = term

                @pl.when(k > start)
                def _():
                    acc[t, half, :] += term

            @pl.when(part == 0)
            def _():
                @pl.loop(0, 4)
                def _(i):
                    core_out[t, rows(i * 64, 64), :] = acc[t, rows((1 - c) * 256 + i * 64, 64), :].astype(BF16)

                core_copy(t).start()

    def core_total(t, off, row, size):
        i = (y + off) % 4 * 64 + row
        return acc[t, rows(c * 256 + i, size), :] + core_in[t, rows(i, size), :].astype(F32)

    def over_cores(t):
        core_copy(t).wait_recv()
        for leap in (0, 1, 2, 3):
            off, row, _, _ = LEAPS[leap]
            y_out[t, rows((y + off) % 4 * 64 + row, 32), :] = core_total(t, off, row, 32).astype(BF16)
            y_copy(t, leap).start()
        y_own[t] = core_total(t, 0, 0, 64)

    def over_half(t):
        for leap in (4, 5):
            off, row, _, _ = LEAPS[leap]
            y_copy(t, leap - 4).wait_recv()
            total = core_total(t, off, row, 32) + y_half[t, leap - 4].astype(F32)
            y_out[t, rows((y + off) % 4 * 64 + row, 32), :] = total.astype(BF16)
            y_copy(t, leap).start()

    def z_copy(t, step):
        q = nibble(w_piece, t)
        to = (zh + step) % 4
        place = nibble(w_place, t)
        return remote(
            z_out.at[t, rows(to * 16, 16)], z_in.at[q % PIECES, place, zh], s_z.at[t, step],
            r_z.at[q % PIECES, place, zh], device(q // PIECES, to, y, c),
        )

    def over_y(t):
        for leap in (2, 3, 4, 5):
            y_copy(t, leap).wait_recv()
        total = y_own[t] + y_in[t, 0].astype(F32) + y_in[t, 1].astype(F32)
        z_out[t] = total.astype(BF16)
        y_own[t] = total
        for step in (2, 1, 3):
            z_copy(t, step).start()
        q = nibble(w_piece, t)

        @pl.when(q // PIECES != me)
        def _():
            z_copy(t, 0).start()

        @pl.when(q // PIECES == me)
        def _():
            z_own[q % PIECES] = y_own[t, rows(zh * 16, 16), :]

    @pl.loop(0, n_steps)
    def _(i):
        kind, t = nibble(w_kind, i), nibble(w_step, i)
        for at, act in enumerate((multiply, over_cores, over_half, over_y)):

            @pl.when(kind == at)
            def _():
                act(t)

    def recv_z(h, a, from_zh):
        got = z_in.at[h, a, from_zh]
        return remote(got, got, s_z.at[0, 0], r_z.at[h, a, from_zh], device(me, zh, y, 1 - c))

    for h in range(PIECES):
        for step in (1, 2, 3):
            recv_z(h, 0, (zh + step) % 4).wait_recv()
            z_own[h] += z_in[h, 0, (zh + step) % 4].astype(F32)

        @pl.loop(1, pick(me, [len(tab.adders[m * PIECES + h]) for m in range(len(tab.nslots))]))
        def _(a):
            for step in range(4):
                recv_z(h, a, step).wait_recv()
                z_own[h] += z_in[h, a, step].astype(F32)

        part = slice(h * width, (h + 1) * width)
        out[0, :, part] = (z_own[h] + dec_bias[:, part]).astype(BF16)

    for step in (1, 2, 3):
        gather_z(step).wait_send()
        for off in range(4):
            gather_y(step, off).wait_send()
    for step in range(4):
        for off in range(4):
            gather_c(step, off).wait_send()

    @pl.loop(0, n_dec)
    def _(j):
        send_dec(j).wait_send()

    @pl.loop(0, n_lat)
    def _(i):
        send_latent(i, 0).wait_send()
        send_latent(i, 1).wait_send()

    @pl.loop(0, n_slots)
    def _(t):
        core_copy(t).wait_send()
        for leap in range(6):
            y_copy(t, leap).wait_send()
        for step in (1, 2, 3):
            z_copy(t, step).wait_send()

        @pl.when(nibble(w_piece, t) // PIECES != me)
        def _():
            z_copy(t, 0).wait_send()


def solution(mesh):
    tab = Tables(PLAN)
    n_lat = 1 + max(len(s) for s in tab.sources)
    T, K, A = tab.slots, tab.depth, tab.most_adders
    J = max(max(len(d) for d in tab.dec), 1)
    N = max(max(len(d) for d in tab.lat), 1)
    DMA = pltpu.SemaphoreType.DMA

    def local(acts, enc_weight, enc_bias, dec_weight, dec_bias):
        whole = acts.shape[2]
        width = whole // PIECES
        return pl.pallas_call(
            functools.partial(kernel, tab),
            out_shape=jax.ShapeDtypeStruct((1, 16, whole), BF16),
            in_specs=[
                pl.BlockSpec(memory_space=pl.ANY),
                pl.BlockSpec(memory_space=pl.ANY),
                pl.BlockSpec(memory_space=pltpu.VMEM),
                pl.BlockSpec(memory_space=pl.ANY),
                pl.BlockSpec(memory_space=pltpu.VMEM),
            ],
            out_specs=pl.BlockSpec(memory_space=pltpu.VMEM),
            scratch_shapes=[
                pltpu.VMEM((512, whole), BF16),
                pltpu.VMEM((whole, 256), BF16),
                pltpu.VMEM((n_lat, 512, 256), BF16),
                pltpu.VMEM((K, 256, width), BF16),
                pltpu.VMEM((T, 512, width), F32),
                pltpu.VMEM((T, 256, width), BF16),
                pltpu.VMEM((T, 256, width), BF16),
                pltpu.VMEM((T, 256, width), BF16),
                pltpu.VMEM((T, 2, 32, width), BF16),
                pltpu.VMEM((T, 64, width), F32),
                pltpu.VMEM((T, 2, 64, width), BF16),
                pltpu.VMEM((T, 64, width), BF16),
                pltpu.VMEM((PIECES, 16, width), F32),
                pltpu.VMEM((PIECES, A, 4, 16, width), BF16),
                DMA((2,)),
                DMA((K,)),
                DMA((J,)),
                DMA((K,)),
                DMA((N, 2)),
                DMA((n_lat, 2)),
                DMA((3,)),
                DMA((3,)),
                DMA((3, 4)),
                DMA((3, 4)),
                DMA((4, 4)),
                DMA((4, 4)),
                DMA((T,)),
                DMA((T,)),
                DMA((T, 6)),
                DMA((T, 6)),
                DMA((T, 4)),
                DMA((PIECES, A, 4)),
            ],
            compiler_params=pltpu.CompilerParams(
                collective_id=0, has_side_effects=True, vmem_limit_bytes=60 * 2**20
            ),
        )(acts, enc_weight, enc_bias, dec_weight, dec_bias)

    return jax.shard_map(
        local,
        mesh=mesh,
        in_specs=(
            P("layer", "lat", None),
            P("layer", None, "lat"),
            P("layer", "lat"),
            P("layer", None, "lat", None),
            P("layer", None),
        ),
        out_specs=P("layer", "lat", None),
        check_vma=False,
    )
```

```python
import functools

import jax
import jax.numpy as jnp
from jax import lax
from jax.experimental import pallas as pl
from jax.experimental.pallas import tpu as pltpu
from jax.sharding import PartitionSpec as P

PLAN = [
    [(1, [(0, 1)]), (0, [(0, 1)]), (3, [(0, 1), (1, 1)]), (7, [(0, 1), (3, 1)])],
    [(1, [(1, 1)]), (2, [(1, 1), (0, 1)]), (7, [(1, 1), (2, 1)])],
    [(4, [(2, 1)]), (2, [(2, 1)]), (5, [(2, 1), (1, 1)])],
    [(6, [(3, 1)]), (5, [(3, 1), (0, 1)]), (3, [(3, 1), (2, 1)])],
    [(5, [(4, 1)]), (6, [(4, 1)]), (4, [(4, 1), (0, -1), (1, -1), (3, -1)])],
    [(7, [(5, 1)]), (5, [(5, 1)]), (6, [(5, 1), (1, 1), (0, 1), (2, 1)])],
    [(6, [(6, 1)])],
    [(7, [(7, 1), (4, 1), (6, 1)])],
]
ORDER = [
    [0, 1, 16, 17, 32, 2, 3, 18, 33, 19, 48, 34, 49, 35, 50, 51],
    [0, 16, 32, 1, 2, 17, 48, 18, 33, 34, 49, 50],
    [0, 1, 16, 17, 32, 2, 33, 18, 48, 49, 34, 50],
    [0, 16, 32, 1, 2, 17, 48, 18, 33, 34, 49, 50],
    [0, 1, 16, 17, 32, 33, 48, 2, 49, 18, 34, 50],
    [0, 1, 16, 17, 32, 33, 48, 2, 49, 18, 34, 50],
    [0, 16, 32, 48],
    [0, 16, 32, 48],
]

F32, BF16 = jnp.float32, jnp.bfloat16
MESH = pl.DeviceIdType.MESH


PIECES = 1


class Tables:
    def __init__(self, plan):
        n = len(plan)
        layers = range(n)
        self.tasks = [[(l, z, q, t) for t, (q, ls) in enumerate(plan[p]) for l, z in ls] for p in layers]
        self.slots = max(len(plan[p]) for p in layers)
        self.depth = max(len(k) for k in self.tasks)
        self.nslots = [len(plan[p]) for p in layers]
        self.piece = [[q for q, _ in plan[p]] for p in layers]
        self.start = [[min(k for k, task in enumerate(self.tasks[p]) if task[3] == t) for t in range(len(plan[p]))] for p in layers]
        self.stop = [[max(k for k, task in enumerate(self.tasks[p]) if task[3] == t) + 1 for t in range(len(plan[p]))] for p in layers]
        self.sources = []
        for p in layers:
            seen = []
            for l, z, _, _ in self.tasks[p]:
                if l != p and (l, z) not in seen:
                    seen.append((l, z))
            self.sources.append(seen)
        self.task_latent = [[0 if l == p else 1 + self.sources[p].index((l, z)) for l, z, _, _ in self.tasks[p]] for p in layers]
        self.task_new = [[int(s > 0 and s not in self.task_latent[p][:k]) for k, s in enumerate(self.task_latent[p])] for p in layers]
        self.task_piece = [[q for _, _, q, _ in self.tasks[p]] for p in layers]
        self.dec = [[(p, z, q, k) for k in range(self.depth) for p in layers for kk, (a, z, q, _) in enumerate(self.tasks[p]) if a == l != p and kk == k] for l in layers]
        for l in layers:
            self.dec[l].sort(key=lambda d: d[0] // 4 != l // 4)
        self.near = [sum(d[0] // 4 == l // 4 for d in self.dec[l]) for l in layers]
        self.lat = [[(p, z, 1 + s) for p in layers for s, (a, z) in enumerate(self.sources[p]) if a == l] for l in layers]
        self.adders = [[q // PIECES] + [p for p in layers if p != q // PIECES and q in self.piece[p]] for q in range(n * PIECES)]
        self.most_adders = max(len(a) for a in self.adders)
        self.adder_place = [[self.adders[q].index(p) for q in self.piece[p]] for p in layers]
        self.adds_to = [[m for m in layers if m != p and any(q // PIECES == m for q in self.piece[p])] for p in layers]
        self.added_by = [[p for p in layers if m in self.adds_to[p]] for m in layers]
        for p in layers:
            assert all(p * PIECES + h in self.piece[p] for h in range(PIECES)) and len(self.tasks[p]) <= 16


def word(values):
    total = sum(v << (4 * i) for i, v in enumerate(values))
    return total - (1 << 32) if total >= 1 << 31 else total


def pick(index, values):
    result = jnp.int32(values[0])
    for i, value in enumerate(values[1:], 1):
        result = jnp.where(index == i, jnp.int32(value), result)
    return result


def words(index, lists):
    most = max(len(values) for values in lists)
    return [pick(index, [word(values[at : at + 8]) for values in lists]) for at in range(0, max(most, 1), 8)]


def nibble(packed, i):
    chosen = packed[0]
    for at, other in enumerate(packed[1:], 1):
        chosen = jnp.where(i >= 8 * at, other, chosen)
    return lax.bitwise_and(lax.shift_right_logical(chosen, jnp.int32(4 * (i % 8))), jnp.int32(15))


def kernel(
    tab, acts, enc, enc_bias, dec, dec_bias, out,
    every, enc_v, latents, decs, acc, core_out, core_in, y_out, y_half, y_own, y_in, z_out, z_own, z_in,
    s_in, s_dec, s_task, r_task, s_lat, r_lat, s_gz, r_gz, s_gy, r_gy, s_gc, r_gc,
    s_core, r_core, s_y, r_y, s_z, r_z,
):
    me = lax.axis_index("layer")
    lat = lax.axis_index("lat")
    zh, y, c = lat // 8, (lat // 2) % 4, lat % 2
    width = acts.shape[2] // PIECES

    def device(layer, zh_, y_, c_):
        return (layer, (zh_ % 4) * 8 + (y_ % 4) * 2 + c_)

    def remote(src, dst, send, recv, where):
        return pltpu.make_async_remote_copy(
            src_ref=src, dst_ref=dst, send_sem=send, recv_sem=recv, device_id=where, device_id_type=MESH
        )

    def rows(start, size):
        return pl.ds(pl.multiple_of(start, 16), size)

    n_slots = pick(me, tab.nslots)
    n_tasks = pick(me, [len(k) for k in tab.tasks])
    w_piece = words(me, tab.piece)
    w_start = words(me, tab.start)
    w_stop = words(me, tab.stop)
    n_steps = pick(me, [len(o) for o in ORDER])
    w_kind = words(me, [[v // 16 for v in o] for o in ORDER])
    w_step = words(me, [[v % 16 for v in o] for o in ORDER])
    w_task_lat = words(me, tab.task_latent)
    w_task_new = words(me, tab.task_new)
    w_task_q = words(me, tab.task_piece)
    n_dec = pick(me, [len(d) for d in tab.dec])
    n_near = pick(me, tab.near)
    w_dec_p = words(me, [[d[0] for d in ds] for ds in tab.dec])
    w_dec_z = words(me, [[int(d[1] < 0) for d in ds] for ds in tab.dec])
    w_dec_q = words(me, [[d[2] for d in ds] for ds in tab.dec])
    w_dec_k = words(me, [[d[3] for d in ds] for ds in tab.dec])
    n_lat = pick(me, [len(d) for d in tab.lat])
    w_lat_p = words(me, [[d[0] for d in ds] for ds in tab.lat])
    w_lat_z = words(me, [[int(d[1] < 0) for d in ds] for ds in tab.lat])
    w_lat_s = words(me, [[d[2] for d in ds] for ds in tab.lat])
    n_src = pick(me, [len(d) for d in tab.sources])
    w_src_l = words(me, [[d[0] for d in ds] for ds in tab.sources])
    w_src_z = words(me, [[int(d[1] < 0) for d in ds] for ds in tab.sources])
    n_to = pick(me, [len(d) for d in tab.adds_to])
    n_by = pick(me, [len(d) for d in tab.added_by])
    w_by = words(me, tab.added_by)
    w_place = words(me, tab.adder_place)

    def columns(q):
        return pl.ds(pl.multiple_of((q % PIECES) * width, 128), width)

    def dec_of(q):
        return dec.at[0, q // PIECES, :, columns(q)]

    own_block = c * 16 + y * 4 + zh
    in_acts = pltpu.make_async_copy(acts.at[0], every.at[rows(own_block * 16, 16)], s_in.at[0])
    in_enc = pltpu.make_async_copy(enc.at[0], enc_v, s_in.at[1])
    in_acts.start()
    in_enc.start()

    def local_dec(k):
        return pltpu.make_async_copy(dec_of(nibble(w_task_q, k)), decs.at[k], s_dec.at[k])

    @pl.loop(0, n_tasks)
    def _(k):
        @pl.when(nibble(w_task_lat, k) == 0)
        def _():
            local_dec(k).start()

    barrier = pltpu.get_barrier_semaphore()

    def greet(where):
        pl.semaphore_signal(barrier, inc=1, device_id=where, device_id_type=MESH)

    greet(device(me, zh, y, 1 - c))
    for step in (1, 3):
        greet(device(me, zh + step, y, c))
    for step in (1, 2, 3):
        greet(device(me, zh, y + step, c))

    @pl.loop(0, n_src)
    def _(i):
        greet(device(nibble(w_src_l, i), zh + nibble(w_src_z, i), y, c))

    @pl.loop(0, n_by)
    def _(i):
        greet(device(nibble(w_by, i), zh, y, c))

    in_acts.wait()
    pl.semaphore_wait(barrier, 6 + n_lat + n_to)

    def block(from_y, from_zh):
        return every.at[rows((c * 16 + (from_y % 4) * 4 + from_zh % 4) * 16, 16)]

    def gather_z(step):
        part = block(y, zh + 3 if step == 2 else zh)
        return remote(part, part, s_gz.at[step - 1], r_gz.at[step - 1], device(me, zh + (1 if step == 2 else step), y, c))

    def gather_y(step, off):
        part = block(y, zh + off)
        return remote(part, part, s_gy.at[step - 1, off], r_gy.at[step - 1, off], device(me, zh, y + step, c))

    def gather_c(step, off):
        part = block(y + 4 - step, zh + off)
        return remote(part, part, s_gc.at[step, off], r_gc.at[step, off], device(me, zh, y, 1 - c))

    def spread(off):
        for step in (2, 1, 3):
            gather_y(step, off).start()
        gather_c(0, off).start()

    gather_z(1).start()
    gather_z(3).start()
    spread(0)

    def send_dec(j):
        k = nibble(w_dec_k, j)
        return remote(
            dec_of(nibble(w_dec_q, j)), decs.at[k], s_task.at[j], r_task.at[k],
            device(nibble(w_dec_p, j), zh + 4 - nibble(w_dec_z, j), y, c),
        )

    @pl.loop(0, n_near)
    def _(j):
        send_dec(j).start()

    gather_z(1).wait_recv()
    gather_z(2).start()
    spread(3)
    gather_z(3).wait_recv()
    spread(1)

    @pl.loop(n_near, n_dec)
    def _(j):
        send_dec(j).start()

    gather_z(2).wait_recv()
    spread(2)

    for off in (0, 3, 1, 2):
        for step in (1, 3, 2):
            gather_y(step, off).wait_recv()
            gather_c(step, off).start()
    in_enc.wait()

    def encode(half):
        pre = jnp.dot(every[rows(half * 256, 256), :], enc_v[...], preferred_element_type=F32) + enc_bias[...]
        latents[0, rows(half * 256, 256), :] = jnp.maximum(pre, 0.0).astype(BF16)

    def send_latent(i, part):
        half = c if part == 0 else 1 - c
        s = nibble(w_lat_s, i)
        return remote(
            latents.at[0, rows(half * 256, 256)], latents.at[s, rows(half * 256, 256)],
            s_lat.at[i, part], r_lat.at[s, part],
            device(nibble(w_lat_p, i), zh + 4 - nibble(w_lat_z, i), y, c),
        )

    encode(c)

    @pl.loop(0, n_lat)
    def _(i):
        send_latent(i, 0).start()

    for step in range(4):
        for off in range(4):
            gather_c(step, off).wait_recv()
    encode(1 - c)

    @pl.loop(0, n_lat)
    def _(i):
        send_latent(i, 1).start()

    def recv_latent(s, part):
        half = c if part == 0 else 1 - c
        block = latents.at[s, rows(half * 256, 256)]
        return remote(block, block, s_lat.at[0, part], r_lat.at[s, part], device(me, zh, y, 1 - c))

    def recv_dec(k):
        return remote(decs.at[k], decs.at[k], s_task.at[0], r_task.at[k], device(me, zh, y, 1 - c))

    def core_copy(t):
        return remote(core_out.at[t], core_in.at[t], s_core.at[t], r_core.at[t], device(me, zh, y, 1 - c))

    LEAPS = ((2, 0, 1, 0), (2, 32, 3, 1), (1, 32, 1, 2), (3, 0, 3, 3), (1, 0, 1, 4), (3, 32, 3, 5))

    def y_copy(t, leap):
        off, row, step, sem = LEAPS[leap]
        place = 0 if step == 1 else 1
        dst = y_half.at[t, place] if leap < 2 else y_in.at[t, place, pl.ds(row, 32)]
        return remote(
            y_out.at[t, rows(((y + off) % 4) * 64 + row, 32)], dst,
            s_y.at[t, sem], r_y.at[t, sem], device(me, zh, y + step, c),
        )

    def multiply(t):
        start, stop = nibble(w_start, t), nibble(w_stop, t)

        @pl.loop(start, stop)
        def _(k):
            s = nibble(w_task_lat, k)

            @pl.when(s == 0)
            def _():
                local_dec(k).wait()

            @pl.when(nibble(w_task_new, k) == 1)
            def _():
                recv_latent(s, 0).wait_recv()
                recv_latent(s, 1).wait_recv()

            @pl.when(s > 0)
            def _():
                recv_dec(k).wait_recv()

        @pl.loop(0, 2)
        def _(part):
            half = rows((c + 1 + part) % 2 * 256, 256)

            @pl.loop(start, stop)
            def _(k):
                s = nibble(w_task_lat, k)
                term = jnp.dot(latents[s, half, :], decs[k], preferred_element_type=F32)

                @pl.when(k == start)
                def _():
                    acc[t, half, :] = term

                @pl.when(k > start)
                def _():
                    acc[t, half, :] += term

            @pl.when(part == 0)
            def _():
                @pl.loop(0, 4)
                def _(i):
                    core_out[t, rows(i * 64, 64), :] = acc[t, rows((1 - c) * 256 + i * 64, 64), :].astype(BF16)

                core_copy(t).start()

    def core_total(t, off, row, size):
        i = (y + off) % 4 * 64 + row
        return acc[t, rows(c * 256 + i, size), :] + core_in[t, rows(i, size), :].astype(F32)

    def over_cores(t):
        core_copy(t).wait_recv()
        for leap in (0, 1, 2, 3):
            off, row, _, _ = LEAPS[leap]
            y_out[t, rows((y + off) % 4 * 64 + row, 32), :] = core_total(t, off, row, 32).astype(BF16)
            y_copy(t, leap).start()
        y_own[t] = core_total(t, 0, 0, 64)

    def over_half(t):
        for leap in (4, 5):
            off, row, _, _ = LEAPS[leap]
            y_copy(t, leap - 4).wait_recv()
            total = core_total(t, off, row, 32) + y_half[t, leap - 4].astype(F32)
            y_out[t, rows((y + off) % 4 * 64 + row, 32), :] = total.astype(BF16)
            y_copy(t, leap).start()

    def z_copy(t, step):
        q = nibble(w_piece, t)
        to = (zh + step) % 4
        place = nibble(w_place, t)
        return remote(
            z_out.at[t, rows(to * 16, 16)], z_in.at[q % PIECES, place, zh], s_z.at[t, step],
            r_z.at[q % PIECES, place, zh], device(q // PIECES, to, y, c),
        )

    def over_y(t):
        for leap in (2, 3, 4, 5):
            y_copy(t, leap).wait_recv()
        total = y_own[t] + y_in[t, 0].astype(F32) + y_in[t, 1].astype(F32)
        z_out[t] = total.astype(BF16)
        y_own[t] = total
        for step in (2, 1, 3):
            z_copy(t, step).start()
        q = nibble(w_piece, t)

        @pl.when(q // PIECES != me)
        def _():
            z_copy(t, 0).start()

        @pl.when(q // PIECES == me)
        def _():
            z_own[q % PIECES] = y_own[t, rows(zh * 16, 16), :]

    @pl.loop(0, n_steps)
    def _(i):
        kind, t = nibble(w_kind, i), nibble(w_step, i)
        for at, act in enumerate((multiply, over_cores, over_half, over_y)):

            @pl.when(kind == at)
            def _():
                act(t)

    def recv_z(h, a, from_zh):
        got = z_in.at[h, a, from_zh]
        return remote(got, got, s_z.at[0, 0], r_z.at[h, a, from_zh], device(me, zh, y, 1 - c))

    for h in range(PIECES):
        for step in (1, 2, 3):
            recv_z(h, 0, (zh + step) % 4).wait_recv()
            z_own[h] += z_in[h, 0, (zh + step) % 4].astype(F32)

        @pl.loop(1, pick(me, [len(tab.adders[m * PIECES + h]) for m in range(len(tab.nslots))]))
        def _(a):
            for step in range(4):
                recv_z(h, a, step).wait_recv()
                z_own[h] += z_in[h, a, step].astype(F32)

        part = slice(h * width, (h + 1) * width)
        out[0, :, part] = (z_own[h] + dec_bias[:, part]).astype(BF16)

    for step in (1, 2, 3):
        gather_z(step).wait_send()
        for off in range(4):
            gather_y(step, off).wait_send()
    for step in range(4):
        for off in range(4):
            gather_c(step, off).wait_send()

    @pl.loop(0, n_dec)
    def _(j):
        send_dec(j).wait_send()

    @pl.loop(0, n_lat)
    def _(i):
        send_latent(i, 0).wait_send()
        send_latent(i, 1).wait_send()

    @pl.loop(0, n_slots)
    def _(t):
        core_copy(t).wait_send()
        for leap in range(6):
            y_copy(t, leap).wait_send()
        for step in (1, 2, 3):
            z_copy(t, step).wait_send()

        @pl.when(nibble(w_piece, t) // PIECES != me)
        def _():
            z_copy(t, 0).wait_send()


def solution(mesh):
    tab = Tables(PLAN)
    n_lat = 1 + max(len(s) for s in tab.sources)
    T, K, A = tab.slots, tab.depth, tab.most_adders
    J = max(max(len(d) for d in tab.dec), 1)
    N = max(max(len(d) for d in tab.lat), 1)
    DMA = pltpu.SemaphoreType.DMA

    def local(acts, enc_weight, enc_bias, dec_weight, dec_bias):
        whole = acts.shape[2]
        width = whole // PIECES
        return pl.pallas_call(
            functools.partial(kernel, tab),
            out_shape=jax.ShapeDtypeStruct((1, 16, whole), BF16),
            in_specs=[
                pl.BlockSpec(memory_space=pl.ANY),
                pl.BlockSpec(memory_space=pl.ANY),
                pl.BlockSpec(memory_space=pltpu.VMEM),
                pl.BlockSpec(memory_space=pl.ANY),
                pl.BlockSpec(memory_space=pltpu.VMEM),
            ],
            out_specs=pl.BlockSpec(memory_space=pltpu.VMEM),
            scratch_shapes=[
                pltpu.VMEM((512, whole), BF16),
                pltpu.VMEM((whole, 256), BF16),
                pltpu.VMEM((n_lat, 512, 256), BF16),
                pltpu.VMEM((K, 256, width), BF16),
                pltpu.VMEM((T, 512, width), F32),
                pltpu.VMEM((T, 256, width), BF16),
                pltpu.VMEM((T, 256, width), BF16),
                pltpu.VMEM((T, 256, width), BF16),
                pltpu.VMEM((T, 2, 32, width), BF16),
                pltpu.VMEM((T, 64, width), F32),
                pltpu.VMEM((T, 2, 64, width), BF16),
                pltpu.VMEM((T, 64, width), BF16),
                pltpu.VMEM((PIECES, 16, width), F32),
                pltpu.VMEM((PIECES, A, 4, 16, width), BF16),
                DMA((2,)),
                DMA((K,)),
                DMA((J,)),
                DMA((K,)),
                DMA((N, 2)),
                DMA((n_lat, 2)),
                DMA((3,)),
                DMA((3,)),
                DMA((3, 4)),
                DMA((3, 4)),
                DMA((4, 4)),
                DMA((4, 4)),
                DMA((T,)),
                DMA((T,)),
                DMA((T, 6)),
                DMA((T, 6)),
                DMA((T, 4)),
                DMA((PIECES, A, 4)),
            ],
            compiler_params=pltpu.CompilerParams(
                collective_id=0, has_side_effects=True, vmem_limit_bytes=60 * 2**20
            ),
        )(acts, enc_weight, enc_bias, dec_weight, dec_bias)

    return jax.shard_map(
        local,
        mesh=mesh,
        in_specs=(
            P("layer", "lat", None),
            P("layer", None, "lat"),
            P("layer", "lat"),
            P("layer", None, "lat", None),
            P("layer", None),
        ),
        out_specs=P("layer", "lat", None),
        check_vma=False,
    )
```
